256 devices in a mesh: rows: 32 (over z, y), days: 8 (over x, core).
Axes of the slice: x: 4, y: 4, z: 8, core: 2. Of those that a mesh axis runs over, the one named last changes fastest.
Arguments:
- observations: float32 [256, 128, 1024], P('days', 'rows'), may hold values from -12 to 12, as said below
- obs_mask: int32 [256, 128, 1024], P('days', 'rows'), may hold values 0 or 1
- obs_weight: float32 [128, 1024], P('rows'), may hold values from 0.5 to 4
- classes: int32 [128, 1024], P('rows'), may hold values from 0 to 15
- kappa_table: float32 [16], replicated, may hold values from 0.02 to 2
Outputs:
- solution: float32 [256, 128, 1024], P('days', 'rows')
- residual: float32 [256, 128, 1024], P('days', 'rows')
The draws below stay inside these ranges and needn't reach their ends.
Inputs may be any that keep to these rules, and one draw needn't show every extreme that they name: `observations`: observed values, given at every cell and day whether observed or not.
All inputs are finite; a program needn't handle non-finite values. No bound on the sum of `obs_mask` on one device may be relied on, other than what follows from the above.
Results may differ from the reference program's by a relative error of at most 0.0003.
Values sent between devices are 32-bit elements; how exact they have to be, the bound alone decides.
A program may use at most 64 MiB of HBM per device.

```python
import math
import jax
import jax.numpy as jnp
from jax import lax

NT = 256
NCLASS = 16
DEG = 8
ITERS = 2
NY = 1024
NX = 128


def draw_observations(key, part):
    key = jax.random.fold_in(key, 11)
    rowpos = jnp.arange(NX, dtype=jnp.float32) / max(NX - 1, 1)
    rising = (1.0 + 2.0 * rowpos)[None, :, None]
    rough = jnp.clip(jax.random.normal(key, (NT, NX, NY), jnp.float32), -3.9, 3.9)
    return rough * rising


def plant(values, stream_key, smallest, largest):
    extent = values.shape
    spot = [jax.random.randint(jax.random.fold_in(stream_key, axis), (), 0, extent[axis]) for axis in range(len(extent))]
    values = values.at[tuple(spot)].set(smallest)
    longest = extent.index(max(extent))
    spot[longest] = (spot[longest] + 1) % extent[longest]
    return values.at[tuple(spot)].set(largest)


def levels(rng, dims, split, least, largest):
    def one(axis_at, shards_of):
        draws = jax.random.uniform(jax.random.fold_in(jax.random.fold_in(rng, 6), axis_at), (shards_of,), jnp.float32, least / len(split), largest / len(split))
        return jnp.repeat(jnp.exp(draws), dims[axis_at] // shards_of).reshape((-1,) + (1,) * (len(dims) - axis_at - 1))

    level = one(*split[0])
    for cut in split[1:]:
        level = level * one(*cut)
    return level


def setup_inputs(seed: int = 0) -> dict:
    keys = jax.random.split(jax.random.key(seed), 6)
    observations = draw_observations(jax.random.fold_in(keys[5], 71), 0)
    obs_mask = plant((jax.random.randint(keys[1], (NT, NX, NY), 0, 2) < 1).astype(jnp.int32), jax.random.fold_in(keys[1], 1), 0, 1)
    obs_weight = jnp.clip(jnp.exp(math.log(4.0) - 2.0794415 * jax.random.uniform(keys[2], (NX, NY), jnp.float32) ** levels(keys[2], (NX, NY), ((0, 32),), -0.2, 0.2)), 0.5, 4.0)
    classes = plant(jax.random.randint(keys[3], (NX, NY), 0, NCLASS), jax.random.fold_in(keys[3], 1), 0, NCLASS - 1).astype(jnp.int32)
    kappa_table = jnp.clip(jnp.exp(jax.random.uniform(keys[4], (NCLASS,), jnp.float32, math.log(0.02), math.log(2.0))), 0.02, 2.0)
    return {"observations": observations, "obs_mask": obs_mask, "obs_weight": obs_weight, "classes": classes, "kappa_table": kappa_table}


TIME_SHIFT = 0.05
HALF_OBS = 0.5
KAPPA_LOW = 0.02
KAPPA_HIGH = 2.0
WEIGHT_LOW = 0.5
WEIGHT_HIGH = 4.0
CENTRE_WEIGHT = 20.0 / 6.0
EDGE_WEIGHT = 4.0 / 6.0
CORNER_WEIGHT = 1.0 / 6.0
STENCIL_TOP = 16.0 / 3.0

def time_basis(first, count, total):
    moment = jnp.arange(count, dtype=jnp.int32) + first
    orders = jnp.arange(total, dtype=jnp.int32)
    phase = (moment[:, None] + 1) * (orders[None, :] + 1) % (2 * (total + 1))
    return jnp.sqrt(2.0 / (total + 1)) * jnp.sin(jnp.pi * phase.astype(jnp.float32) / (total + 1))

def mode_eigs(first, count, total):
    orders = (jnp.arange(count, dtype=jnp.int32) + first + 1).astype(jnp.float32)
    return 2.0 + TIME_SHIFT - 2.0 * jnp.cos(jnp.pi * orders / (total + 1))

def nine_point(padded, core):
    framed = jnp.pad(padded, ((0, 0), (0, 0), (1, 1)))
    edges = framed[:, :-2, 1:-1] + framed[:, 2:, 1:-1] + framed[:, 1:-1, :-2] + framed[:, 1:-1, 2:]
    corners = framed[:, :-2, :-2] + framed[:, :-2, 2:] + framed[:, 2:, :-2] + framed[:, 2:, 2:]
    return CENTRE_WEIGHT * core - EDGE_WEIGHT * edges - CORNER_WEIGHT * corners

def chebyshev(rhs, eigen_vals, apply_fn):
    lower = eigen_vals * KAPPA_LOW + HALF_OBS * WEIGHT_LOW
    upper = eigen_vals * (KAPPA_HIGH + STENCIL_TOP) + HALF_OBS * WEIGHT_HIGH
    centre = 0.5 * (upper + lower)
    spread = 0.5 * (upper - lower)
    stretch = centre / spread
    ratio = 1.0 / stretch
    result = jnp.zeros_like(rhs)
    remainder = rhs
    update = rhs / centre
    for sweep in range(DEG):
        result = result + update
        if sweep + 1 < DEG:
            remainder = remainder - apply_fn(update)
            ratio_next = 1.0 / (2.0 * stretch - ratio)
            update = ratio_next * ratio * update + 2.0 * ratio_next / spread * remainder
            ratio = ratio_next
    return result

def reference(observations, obs_mask, obs_weight, classes, kappa_table):
    total = observations.shape[0]
    kappa_cell = kappa_table[classes]
    seen_weight = obs_mask.astype(jnp.float32) * obs_weight
    rhs = seen_weight * observations
    basis = time_basis(0, total, total)
    eigen_vals = mode_eigs(0, total, total)[:, None, None]

    def operate(field):
        day_pad = jnp.pad(field, ((1, 1), (0, 0), (0, 0)))
        coupled = (2.0 + TIME_SHIFT) * field - day_pad[:-2] - day_pad[2:]
        padded = jnp.pad(coupled, ((0, 0), (1, 1), (0, 0)))
        return kappa_cell * coupled + nine_point(padded, coupled) + seen_weight * field

    def mode_apply(field):
        padded = jnp.pad(field, ((0, 0), (1, 1), (0, 0)))
        return eigen_vals * (kappa_cell * field + nine_point(padded, field)) + HALF_OBS * obs_weight * field

    def precondition(current):
        modes = jnp.einsum('tk,txy->kxy', basis, current, precision=lax.Precision.HIGHEST)
        smooth = chebyshev(modes, eigen_vals, mode_apply)
        return jnp.einsum('kt,kxy->txy', basis, smooth, precision=lax.Precision.HIGHEST)
    solution = jnp.zeros_like(rhs)
    residual = rhs
    precond = precondition(residual)
    direction = precond
    fit = jnp.sum(residual * precond)
    for step in range(ITERS):
        image = operate(direction)
        alpha = fit / jnp.sum(direction * image)
        solution = solution + alpha * direction
        residual = residual - alpha * image
        if step + 1 < ITERS:
            precond = precondition(residual)
            fit_next = jnp.sum(residual * precond)
            direction = precond + fit_next / fit * direction
            fit = fit_next
    return (solution, residual)
```

```python
import math

import jax
import jax.numpy as jnp
import numpy as np
from jax import lax
from jax.experimental import pallas as pl
from jax.experimental.pallas import tpu as pltpu
from jax.sharding import PartitionSpec as P

MESH = pl.DeviceIdType.MESH
DEG = 8
TIME_SHIFT = 0.05
HALF_OBS = 0.5
KAPPA_LOW = 0.02
KAPPA_HIGH = 2.0
WEIGHT_LOW = 0.5
WEIGHT_HIGH = 4.0
CENTRE_WEIGHT = 20.0 / 6.0
EDGE = 4.0 / 6.0
CORNER = 1.0 / 6.0
STENCIL_TOP = 16.0 / 3.0

Y = 4
TB = 32
RB = 4
COLS = 32
K = 4
LANES = 128


def modal_constants(total):
    order = np.arange(1, total + 1, dtype=np.float64)
    phase = np.outer(order, order) % (2 * (total + 1))
    basis = np.sqrt(2.0 / (total + 1)) * np.sin(np.pi * phase / (total + 1))
    basis = basis.astype(np.float32)
    high = basis.astype(jnp.bfloat16)
    low = (basis - high.astype(np.float32)).astype(jnp.bfloat16)
    eig = 2.0 + TIME_SHIFT - 2.0 * np.cos(np.pi * order / (total + 1))
    lower = eig * KAPPA_LOW + HALF_OBS * WEIGHT_LOW
    upper = eig * (KAPPA_HIGH + STENCIL_TOP) + HALF_OBS * WEIGHT_HIGH
    centre, spread = 0.5 * (upper + lower), 0.5 * (upper - lower)
    rows = np.zeros((8, total), np.float32)
    for at, row in enumerate((eig, 1.0 / centre, centre / spread, 1.0 / spread)):
        rows[at] = row
    return high, low, rows


def make_kernel(Z, D):
    NT = TB * D
    ROWS = RB * Y
    J = Y * D
    WIDE = NT // LANES

    def kernel(
        obs, mask, weight, classes, kappa, bh, bl, modal, sol, res,
        U, R, RES, G, ZH, QH, NAT, NATS, KC, HC, PR, PS, XR, XS,
        TZ, TQ, TW, TV, FZ, FQ, FW, FV, PW, CW, HW, HE, SW, SE, SA, RZ, SG, RG,
        halo_send, halo_recv, all_send, all_recv, cell_send, cell_recv, sum_send, sum_recv,
    ):
        ri, d = lax.axis_index("rows"), lax.axis_index("days")
        z, y = ri // Y, ri % Y
        j = y * D + jnp.where(y % 2 == 0, d, D - 1 - d)
        sub = lax.broadcasted_iota(jnp.int32, (8, NT), 0)

        def place(jt):
            yt, mt = jt // D, jt % D
            return yt, jnp.where(yt % 2 == 0, mt, D - 1 - mt)

        def device(zt, jt):
            yt, dt = place(jt)
            return (zt * Y + yt, dt)

        north, south = lax.rem(z + Z - 1, Z), lax.rem(z + 1, Z)
        west, east = lax.rem(j + J - 1, J), lax.rem(j + 1, J)

        def clear(i, c):
            U[i, 0] = jnp.zeros((K, 8, NT), jnp.float32)
            U[i, ROWS + 1] = jnp.zeros((K, 8, NT), jnp.float32)
            return c

        lax.fori_loop(0, 2, clear, 0)
        HW[...] = jnp.zeros_like(HW)
        HE[...] = jnp.zeros_like(HE)

        barrier = pltpu.get_barrier_semaphore()

        def greet(target):
            pl.semaphore_signal(barrier, inc=1, device_id=target, device_id_type=MESH)

        def greet_plane(i, c):
            greet(device(z, lax.rem(j + i, J)))
            return c

        def greet_column(i, c):
            greet((lax.rem(z + i, Z) * Y + y, d))
            return c

        lax.fori_loop(1, J, greet_plane, 0)
        lax.fori_loop(1, Z, greet_column, 0)
        for zt in (north, south):
            for jt in (west, east):
                greet(device(zt, jt))

        def swap(parts):
            lane = lax.broadcasted_iota(jnp.int32, parts[0].shape, 1)
            wide, even = lane < 64, (lane // 32) % 2 == 0
            t0 = jnp.where(wide, parts[0], pltpu.roll(parts[2], 64, 1))
            t2 = jnp.where(wide, pltpu.roll(parts[0], 64, 1), parts[2])
            t1 = jnp.where(wide, parts[1], pltpu.roll(parts[3], 64, 1))
            t3 = jnp.where(wide, pltpu.roll(parts[1], 64, 1), parts[3])
            d0 = jnp.where(even, t0, pltpu.roll(t1, 32, 1))
            d1 = jnp.where(even, pltpu.roll(t0, 96, 1), t1)
            d2 = jnp.where(even, t2, pltpu.roll(t3, 32, 1))
            d3 = jnp.where(even, pltpu.roll(t2, 96, 1), t3)
            return d0, d1, d2, d3

        slab = pl.ds(pl.multiple_of(d * LANES, LANES), LANES)
        cls = classes[:, slab]
        kap = jnp.zeros((RB, LANES), jnp.float32)
        for level in range(16):
            kap = jnp.where(cls == level, kappa[level], kap)
        own_w = weight[:, slab]
        sub8 = lax.broadcasted_iota(jnp.int32, (8, LANES), 0)
        cells = []
        for r in range(RB):
            w_row = jnp.broadcast_to(own_w[r : r + 1], (8, LANES))
            k_row = jnp.broadcast_to(kap[r : r + 1], (8, LANES))
            cells.append(jnp.where(sub8 == 0, w_row, k_row))
        for q, part in enumerate(swap(cells)):
            PW[q] = part

        pl.semaphore_wait(barrier, (J - 1) + (Z - 1) + 4)

        def cell_copy(q):
            return pltpu.make_async_remote_copy(
                src_ref=PW.at[q], dst_ref=CW.at[y], send_sem=cell_send.at[q],
                recv_sem=cell_recv.at[y], device_id=device(z, 4 * d + q), device_id_type=MESH,
            )

        def cell_local(q):
            return pltpu.make_async_copy(PW.at[q], CW.at[y], cell_recv.at[y])

        for q in range(4):
            @pl.when(4 * d + q != j)
            def _():
                cell_copy(q).start()

            @pl.when(4 * d + q == j)
            def _():
                cell_local(q).start()

        def to_tile(src, dst, at, i):
            jt = lax.rem(j + i, J)
            return pltpu.make_async_remote_copy(
                src_ref=src.at[jt], dst_ref=dst.at[y, pl.ds(pl.multiple_of(d * TB, TB), TB)],
                send_sem=all_send.at[at], recv_sem=all_recv.at[at],
                device_id=device(z, jt), device_id_type=MESH,
            )

        def to_days(src, dst, at, i):
            jt = lax.rem(j + i, J)
            yt, dt = place(jt)
            return pltpu.make_async_remote_copy(
                src_ref=src.at[yt, pl.ds(pl.multiple_of(dt * TB, TB), TB)], dst_ref=dst.at[j],
                send_sem=all_send.at[at], recv_sem=all_recv.at[at],
                device_id=device(z, jt), device_id_type=MESH,
            )

        def send_range(copy, src, dst, at, lo, hi):
            def one(i, c):
                copy(src, dst, at, i).start()
                return c

            lax.fori_loop(lo, hi, one, 0)

        def own_tile(src, dst, at):
            pltpu.make_async_copy(
                src.at[j], dst.at[y, pl.ds(pl.multiple_of(d * TB, TB), TB)], all_recv.at[at]
            ).start()

        def own_days(src, dst, at):
            pltpu.make_async_copy(
                src.at[y, pl.ds(pl.multiple_of(d * TB, TB), TB)], dst.at[j], all_recv.at[at]
            ).start()

        def all_wait(dst, at):
            pltpu.make_async_copy(dst, dst, all_recv.at[at]).wait()

        def all_wait_send(at):
            pltpu.make_async_copy(
                PR.at[pl.ds(0, J - 1)], PR.at[pl.ds(0, J - 1)], all_send.at[at]
            ).wait()

        def shuffle_seen(i, c):
            lanes = pl.ds(pl.multiple_of(i * LANES, LANES), LANES)
            seen, rhs = [], []
            for r in range(RB):
                s = mask[r, :, lanes].astype(jnp.float32) * weight[r : r + 1, lanes]
                seen.append(s)
                rhs.append(s * obs[r, :, lanes])
            for q, part in enumerate(swap(rhs)):
                PR[4 * i + q] = part
            for q, part in enumerate(swap(seen)):
                PS[4 * i + q] = part
            return c

        lax.fori_loop(0, J // 4, shuffle_seen, 0)
        own_tile(PR, XR, 0)
        send_range(to_tile, PR, XR, 0, 1, J)
        own_tile(PS, XS, 1)
        send_range(to_tile, PS, XS, 1, 1, J)

        for yt in range(Y):
            pltpu.make_async_copy(CW.at[yt], CW.at[yt], cell_recv.at[yt]).wait()

        def widen(v):
            return jnp.concatenate([v] * WIDE, axis=-1)

        def spread_cells(at, out, scale, shift):
            for yt in range(Y):
                flat = jnp.broadcast_to(CW[yt][at : at + 1], (LANES, LANES)) * scale + shift
                turned = jnp.transpose(flat).reshape(RB, COLS, LANES)
                NAT[0, yt * RB : (yt + 1) * RB] = turned

            def one(r, c):
                for k in range(K):
                    out[r, k] = NAT[0, r, pl.ds(k, 8, stride=K), :]
                return c

            lax.fori_loop(0, ROWS, one, 0)

        spread_cells(0, HC, HALF_OBS, 0.0)
        spread_cells(1, KC, 1.0, CENTRE_WEIGHT)

        def load_natural(ref, r, k):
            return jnp.concatenate([ref[w, r, pl.ds(k, 8, stride=K), :] for w in range(WIDE)], axis=-1)

        def store_natural(ref, r, k, v):
            for w in range(WIDE):
                ref[w, r, pl.ds(k, 8, stride=K), :] = v[:, w * LANES : (w + 1) * LANES]

        def split(v):
            high = v.astype(jnp.bfloat16)
            return high, (v - high.astype(jnp.float32)).astype(jnp.bfloat16)

        def dot(a, b, dims):
            return lax.dot_general(a, b, (dims, ((), ())), preferred_element_type=jnp.float32)

        def to_modes(tile):
            def one(i, c):
                v = jnp.concatenate([tile(2 * i), tile(2 * i + 1)], axis=1)
                high, low = split(jnp.transpose(v))
                dims = ((1,), (0,))
                h = dot(high, bh[...], dims) + (dot(high, bl[...], dims) + dot(low, bh[...], dims))
                for w in range(WIDE):
                    half = h[:, w * LANES : (w + 1) * LANES]
                    NAT[w, pl.ds(2 * RB * i, 2 * RB)] = half.reshape(2 * RB, COLS, LANES)
                return c

            lax.fori_loop(0, Y // 2, one, 0)

        def to_time(out):
            def one(i, c):
                v = [NATS[w, pl.ds(2 * RB * i, 2 * RB)].reshape(2 * RB * COLS, LANES) for w in range(WIDE)]
                v = jnp.concatenate(v, axis=1)
                high, low = split(v)
                dims = ((1,), (1,))
                t = dot(bh[...], high, dims) + (dot(bl[...], high, dims) + dot(bh[...], low, dims))
                out[2 * i] = t[:, :LANES]
                out[2 * i + 1] = t[:, LANES:]
                return c

            lax.fori_loop(0, Y // 2, one, 0)

        def halo(p):
            def copy(at, src, dst, target):
                return pltpu.make_async_remote_copy(
                    src_ref=src, dst_ref=dst, send_sem=halo_send.at[p, at],
                    recv_sem=halo_recv.at[p, at], device_id=target, device_id_type=MESH,
                )

            top, bottom, left, right = z == 0, z == Z - 1, j == 0, j == J - 1
            dump = ROWS + 2
            far = dump + ROWS
            first = [
                copy(0, U.at[p, 1], U.at[p, jnp.where(top, dump, ROWS + 1)], device(north, j)),
                copy(1, U.at[p, ROWS], U.at[p, jnp.where(bottom, dump, 0)], device(south, j)),
                copy(2, SW.at[p, 0], HE.at[p, jnp.where(top | left, far, ROWS + 1)], device(north, west)),
                copy(3, SE.at[p, 0], HW.at[p, jnp.where(top | right, far, ROWS + 1)], device(north, east)),
                copy(4, SW.at[p, ROWS - 1], HE.at[p, jnp.where(bottom | left, far + 1, 0)], device(south, west)),
                copy(5, SE.at[p, ROWS - 1], HW.at[p, jnp.where(bottom | right, far + 1, 0)], device(south, east)),
            ]
            second = [
                copy(6, SW.at[p], HE.at[p, pl.ds(jnp.where(left, dump, 1), ROWS)], device(z, west)),
                copy(7, SE.at[p], HW.at[p, pl.ds(jnp.where(right, dump, 1), ROWS)], device(z, east)),
            ]
            return first, second

        def halo_wait(p):
            first, second = halo(p)
            for copy in first + second:
                copy.wait()

        def run_rows(q, row, carry):
            first, second = halo(q)
            carry = lax.fori_loop(0, 2, lambda i, c: row(i * (ROWS - 1), c), carry)
            for copy in first:
                copy.start()
            carry = lax.fori_loop(1, ROWS - 1, row, carry)
            for copy in second:
                copy.start()
            return carry

        def put_update(q, r, k, v):
            U[q, r + 1, k] = v
            if k == 0:
                SW[q, r] = v[0:1]
            if k == K - 1:
                SE[q, r] = v[7:8]

        eig = modal[0:1]
        inv_centre = modal[1:2]
        stretch = modal[2:3]
        inv_spread = modal[3:4]

        def apply_row(p, r):
            v = [U[p, r + 1, k] for k in range(K)]
            s = [U[p, r, k] + U[p, r + 2, k] for k in range(K)]
            a = [EDGE * v[k] + CORNER * s[k] for k in range(K)]
            wl = EDGE * HW[p, r + 1] + CORNER * (HW[p, r] + HW[p, r + 2])
            er = EDGE * HE[p, r + 1] + CORNER * (HE[p, r] + HE[p, r + 2])
            before = jnp.where(sub == 0, wl, pltpu.roll(a[K - 1], 1, 0))
            after = jnp.where(sub == 7, er, pltpu.roll(a[0], 7, 0))
            row = [before] + a + [after]
            out = []
            for k in range(K):
                h = row[k] + row[k + 2] + EDGE * s[k]
                hc = widen(HC[r, k])
                out.append((eig * (widen(KC[r, k]) * v[k] - h) + hc * v[k], v[k], hc))
            return out

        def start_row(src):
            def row(r, c):
                for k in range(K):
                    g = load_natural(src, r, k)
                    G[r, k] = g
                    R[r, k] = g
                    u = g * inv_centre
                    RES[r, k] = u
                    put_update(0, r, k, u)
                return c

            return row

        def sweep(p, ratio):
            ratio_next = 1.0 / (2.0 * stretch - ratio)
            ca, cb = ratio_next * ratio, 2.0 * ratio_next * inv_spread

            def row(r, c):
                for k, (dv, v, _) in enumerate(apply_row(p, r)):
                    rem = R[r, k] - dv
                    R[r, k] = rem
                    u = ca * v + cb * rem
                    RES[r, k] = RES[r, k] + u
                    put_update(1 - p, r, k, u)
                return c

            halo_wait(p)
            run_rows(1 - p, row, 0)
            return ratio_next

        def sweeps(lo, hi, ratio, extra=None):
            def one(n, ratio):
                ratio = sweep(n % 2, ratio)
                if extra is not None:
                    extra(n)
                return ratio

            return lax.fori_loop(lo, hi, one, ratio)

        def natural(src):
            def one(r, c):
                for k in range(K):
                    store_natural(NATS, r, k, src[r, k])
                return c

            lax.fori_loop(0, ROWS, one, 0)

        def fold(v):
            v = jnp.sum(v, axis=0, keepdims=True)
            out = v[:, :LANES]
            for i in range(1, WIDE):
                out = out + v[:, i * LANES : (i + 1) * LANES]
            return jnp.broadcast_to(out, (8, LANES))

        def pack(parts):
            out = fold(parts[0])
            for at, part in enumerate(parts[1:], 1):
                out = jnp.where(sub8 == at, fold(part), out)
            return out

        def column_copy(at, i):
            return pltpu.make_async_remote_copy(
                src_ref=SA.at[at], dst_ref=RZ.at[at, z], send_sem=sum_send.at[at, 0],
                recv_sem=sum_recv.at[at, 0],
                device_id=(lax.rem(z + i, Z) * Y + y, d), device_id_type=MESH,
            )

        def plane_copy(at, i):
            return pltpu.make_async_remote_copy(
                src_ref=SG.at[at], dst_ref=RG.at[at, j], send_sem=sum_send.at[at, 1],
                recv_sem=sum_recv.at[at, 1],
                device_id=device(z, lax.rem(j + i, J)), device_id_type=MESH,
            )

        def wait_bytes(ref, count, sem):
            part = ref.at[pl.ds(0, count)]
            pltpu.make_async_copy(part, part, sem).wait()

        def column_start(at, value):
            SA[at] = value
            RZ[at, z] = value

            def one(i, c):
                column_copy(at, i).start()
                return c

            lax.fori_loop(1, Z, one, 0)

        def column_end(at):
            for side in (sum_recv, sum_send):
                wait_bytes(RZ.at[at], Z - 1, side.at[at, 0])
            return lax.fori_loop(1, Z, lambda i, c: c + RZ[at, i], RZ[at, 0])

        def plane_start(at, value):
            SG[at] = value
            RG[at, j] = value

            def one(i, c):
                plane_copy(at, i).start()
                return c

            lax.fori_loop(1, J, one, 0)

        def plane_end(at):
            for side in (sum_recv, sum_send):
                wait_bytes(RG.at[at], J - 1, side.at[at, 1])
            total = lax.fori_loop(1, J, lambda i, c: c + RG[at, i], RG[at, 0])
            return [jnp.sum(total[i : i + 1], axis=1, keepdims=True) for i in range(3)]

        zero = jnp.zeros((8, NT), jnp.float32)

        all_wait(XR, 0)
        to_modes(lambda i: XR[i])
        run_rows(0, start_row(NAT), 0)
        ratio = sweeps(0, DEG - 1, 1.0 / stretch)
        natural(RES)
        to_time(TZ)
        all_wait(XS, 1)
        to_modes(lambda i: TZ[i] * XS[i])
        p = (DEG - 1) % 2

        def first_image(r, acc):
            fit, curve = acc
            for k, (dv, v, hc) in enumerate(apply_row(p, r)):
                g, zh = G[r, k], RES[r, k]
                q = g - (R[r, k] - dv) - hc * zh + load_natural(NAT, r, k)
                ZH[r, k] = zh
                QH[r, k] = q
                store_natural(NATS, r, k, q)
                R[r, k] = q
                u = q * inv_centre
                RES[r, k] = u
                put_update(1 - p, r, k, u)
                fit, curve = fit + g * zh, curve + zh * q
            return fit, curve

        halo_wait(p)
        fit, curve = run_rows(1 - p, first_image, (zero, zero))
        column_start(0, pack([fit, curve]))
        to_time(TQ)
        own_days(TZ, FZ, 2)
        own_days(TQ, FQ, 3)

        def trickle(n):
            lo, hi = 1 + n * (J - 1) // (DEG - 1), 1 + (n + 1) * (J - 1) // (DEG - 1)
            send_range(to_days, TZ, FZ, 2, lo, hi)
            send_range(to_days, TQ, FQ, 3, lo, hi)

        ratio = sweeps(0, 2, 1.0 / stretch, trickle)
        plane_start(0, column_end(0))
        ratio = sweeps(2, DEG - 1, ratio, trickle)
        natural(RES)
        to_time(TW)
        own_days(TW, FW, 4)
        send_range(to_days, TW, FW, 4, 1, J)
        to_modes(lambda i: TW[i] * XS[i])
        fit0, curve0, _ = plane_end(0)
        alpha0 = fit0 / curve0

        def second_image(r, acc):
            fit, curve, cross = acc
            for k, (dv, v, hc) in enumerate(apply_row(p, r)):
                g, wh, zh = QH[r, k], RES[r, k], ZH[r, k]
                q = g - (R[r, k] - dv) - hc * wh + load_natural(NAT, r, k)
                store_natural(NATS, r, k, q)
                z1 = zh - alpha0 * wh
                fit = fit + (G[r, k] - alpha0 * g) * z1
                curve = curve + z1 * (g - alpha0 * q)
                cross = cross + z1 * g
            return fit, curve, cross

        halo_wait(p)
        sums = lax.fori_loop(0, ROWS, second_image, (zero, zero, zero))
        column_start(1, pack(sums))
        to_time(TV)
        own_days(TV, FV, 5)
        send_range(to_days, TV, FV, 5, 1, J)
        plane_start(1, column_end(1))
        fit1, curve1, cross1 = plane_end(1)
        beta = fit1 / fit0
        alpha1 = fit1 / (curve1 + 2.0 * beta * cross1 + beta * beta * curve0)
        c_old = alpha0 + alpha1 + alpha1 * beta
        c_new = alpha0 * alpha1

        for at, dst in ((2, FZ), (3, FQ), (4, FW)):
            all_wait(dst, at)

        def finish(i, c):
            lanes = pl.ds(pl.multiple_of(i * LANES, LANES), LANES)
            for part, out in enumerate((sol, res)):
                values = []
                for q in range(4):
                    at = 4 * i + q
                    if part == 0:
                        values.append(c_old * FZ[at] - c_new * FW[at])
                    else:
                        values.append(PR[at] - c_old * FQ[at] + c_new * FV[at])
                for r, v in enumerate(swap(values)):
                    out[r, :, lanes] = v
            return c

        all_wait(FV, 5)
        lax.fori_loop(0, J // 4, finish, 0)

        for at in range(6):
            all_wait_send(at)
        for q in range(4):
            @pl.when(4 * d + q != j)
            def _():
                cell_copy(q).wait_send()

    f32 = jnp.float32
    field = pltpu.VMEM((ROWS, K, 8, NT), f32)
    flat = pltpu.VMEM((WIDE, ROWS, COLS, LANES), f32)
    cell = pltpu.VMEM((ROWS, K, 8, LANES), f32)
    days = pltpu.VMEM((J, TB, LANES), f32)
    tile = pltpu.VMEM((Y, NT, LANES), f32)
    edge = pltpu.VMEM((2, 2 * ROWS + 4, 1, NT), f32)
    side = pltpu.VMEM((2, ROWS, 1, NT), f32)
    scratch = [
        pltpu.VMEM((2, ROWS + 3, K, 8, NT), f32), field, field, field, field, field, flat, flat,
        cell, cell, days, days, tile, tile, tile, tile, tile, tile, days, days, days, days,
        pltpu.VMEM((4, 8, LANES), f32), pltpu.VMEM((Y, 8, LANES), f32), edge, edge, side, side,
        pltpu.VMEM((2, 8, LANES), f32), pltpu.VMEM((2, Z, 8, LANES), f32),
        pltpu.VMEM((2, 8, LANES), f32), pltpu.VMEM((2, J, 8, LANES), f32),
        pltpu.SemaphoreType.DMA((2, 8)), pltpu.SemaphoreType.DMA((2, 8)),
        pltpu.SemaphoreType.DMA((6,)), pltpu.SemaphoreType.DMA((6,)),
        pltpu.SemaphoreType.DMA((4,)), pltpu.SemaphoreType.DMA((Y,)),
        pltpu.SemaphoreType.DMA((2, 2)), pltpu.SemaphoreType.DMA((2, 2)),
    ]
    return kernel, scratch


def solution(mesh):
    Z = mesh.shape["rows"] // Y
    D = mesh.shape["days"]
    kernel, scratch = make_kernel(Z, D)
    high, low, modal = modal_constants(TB * D)
    vmem = pl.BlockSpec(memory_space=pltpu.VMEM)
    smem = pl.BlockSpec(memory_space=pltpu.SMEM)

    def body(observations, obs_mask, obs_weight, classes, kappa_table):
        shape = jax.ShapeDtypeStruct((RB, TB, COLS * Y * D), jnp.float32)
        sol, res = pl.pallas_call(
            kernel,
            out_shape=(shape, shape),
            in_specs=[vmem] * 4 + [smem] + [vmem] * 3,
            out_specs=(vmem, vmem),
            scratch_shapes=scratch,
            compiler_params=pltpu.CompilerParams(
                collective_id=0, has_side_effects=True, vmem_limit_bytes=48 * 1024 * 1024
            ),
        )(
            jnp.transpose(observations, (1, 0, 2)), jnp.transpose(obs_mask, (1, 0, 2)),
            obs_weight, classes, kappa_table, jnp.asarray(high), jnp.asarray(low), jnp.asarray(modal),
        )
        return jnp.transpose(sol, (1, 0, 2)), jnp.transpose(res, (1, 0, 2))

    in_specs = (P("days", "rows", None), P("days", "rows", None), P("rows", None), P("rows", None), P())
    out_specs = (P("days", "rows", None), P("days", "rows", None))
    return jax.shard_map(body, mesh=mesh, in_specs=in_specs, out_specs=out_specs, check_vma=False)
```

```python
import math

import jax
import jax.numpy as jnp
import numpy as np
from jax import lax
from jax.experimental import pallas as pl
from jax.experimental.pallas import tpu as pltpu
from jax.sharding import PartitionSpec as P

MESH = pl.DeviceIdType.MESH
DEG = 8
TIME_SHIFT = 0.05
HALF_OBS = 0.5
KAPPA_LOW = 0.02
KAPPA_HIGH = 2.0
WEIGHT_LOW = 0.5
WEIGHT_HIGH = 4.0
STENCIL_SCALE = 6.0
STENCIL_TOP = 16.0 / 3.0

Y = 4
TB = 32
RB = 4
COLS = 32
HALO = 8
K = (COLS + 2 * HALO) // 8
LANES = 128


def modal_constants(total):
    order = np.arange(1, total + 1, dtype=np.float64)
    phase = np.outer(order, order) % (2 * (total + 1))
    basis = np.sqrt(2.0 / (total + 1)) * np.sin(np.pi * phase / (total + 1))
    eig = 2.0 + TIME_SHIFT - 2.0 * np.cos(np.pi * order / (total + 1))
    lower = eig * KAPPA_LOW + HALF_OBS * WEIGHT_LOW
    upper = eig * (KAPPA_HIGH + STENCIL_TOP) + HALF_OBS * WEIGHT_HIGH
    centre, spread = 0.5 * (upper + lower), 0.5 * (upper - lower)
    rows = np.zeros((8, total), np.float32)
    for at, row in enumerate((eig / STENCIL_SCALE, 1.0 / centre, centre / spread, 1.0 / spread)):
        rows[at] = row
    return basis.astype(np.float32), rows


def make_kernel(Z, D):
    NT = TB * D
    ROWS = RB * Y
    J = Y * D
    WIDE = NT // LANES
    ER, EC = ROWS + 2 * HALO, COLS + 2 * HALO
    OWN = pl.ds(HALO, COLS)

    def kernel(
        obs, mask, weight, classes, kappa, basis, modal, sol, res,
        GE1, GE2, U, G, KC, HC, NC, MK, NAT, NQ, NZ, NW, NV, PR, PS, XR, XS,
        TZ, TQ, TW, TV, FZ, FQ, FW, FV, PW, CW, CT, CN, SA, RZ, SG, RG,
        halo_send, halo_recv, near_send, near_recv, all_send, all_recv, cell_send, cell_recv,
        sum_send, sum_recv,
    ):
        ri, d = lax.axis_index("rows"), lax.axis_index("days")
        z, y = ri // Y, ri % Y
        j = y * D + jnp.where(y % 2 == 0, d, D - 1 - d)
        top, bottom, left, right = z == 0, z == Z - 1, j == 0, j == J - 1

        def place(jt):
            yt, mt = jt // D, jt % D
            return yt, jnp.where(yt % 2 == 0, mt, D - 1 - mt)

        def device(zt, jt):
            yt, dt = place(jt)
            return (zt * Y + yt, dt)

        north, south = lax.rem(z + Z - 1, Z), lax.rem(z + 1, Z)
        west, east = lax.rem(j + J - 1, J), lax.rem(j + 1, J)

        CN[...] = jnp.zeros_like(CN)
        for cond, rows, cols in (
            (top, pl.ds(0, HALO), pl.ds(0, EC)),
            (bottom, pl.ds(HALO + ROWS, HALO), pl.ds(0, EC)),
            (left, pl.ds(0, ER), pl.ds(0, HALO)),
            (right, pl.ds(0, ER), pl.ds(HALO + COLS, HALO)),
        ):
            @pl.when(cond)
            def _():
                for ge in (GE1, GE2):
                    for w in range(WIDE):
                        ge[w, rows, cols, :] = jnp.zeros((rows.size, cols.size, LANES), jnp.float32)

        barrier = pltpu.get_barrier_semaphore()

        def greet(target):
            pl.semaphore_signal(barrier, inc=1, device_id=target, device_id_type=MESH)

        def greet_plane(i, c):
            greet(device(z, lax.rem(j + i, J)))
            return c

        def greet_column(i, c):
            greet((lax.rem(z + i, Z) * Y + y, d))
            return c

        lax.fori_loop(1, J, greet_plane, 0)
        lax.fori_loop(1, Z, greet_column, 0)
        for zt in (north, south):
            for jt in (west, east):
                greet(device(zt, jt))

        def swap(parts):
            lane = lax.broadcasted_iota(jnp.int32, parts[0].shape, 1)
            wide, even = lane < 64, (lane // 32) % 2 == 0
            t0 = jnp.where(wide, parts[0], pltpu.roll(parts[2], 64, 1))
            t2 = jnp.where(wide, pltpu.roll(parts[0], 64, 1), parts[2])
            t1 = jnp.where(wide, parts[1], pltpu.roll(parts[3], 64, 1))
            t3 = jnp.where(wide, pltpu.roll(parts[1], 64, 1), parts[3])
            d0 = jnp.where(even, t0, pltpu.roll(t1, 32, 1))
            d1 = jnp.where(even, pltpu.roll(t0, 96, 1), t1)
            d2 = jnp.where(even, t2, pltpu.roll(t3, 32, 1))
            d3 = jnp.where(even, pltpu.roll(t2, 96, 1), t3)
            return d0, d1, d2, d3

        slab = pl.ds(pl.multiple_of(d * LANES, LANES), LANES)
        cls = classes[:, slab]
        kap = jnp.zeros((RB, LANES), jnp.float32)
        for level in range(16):
            kap = jnp.where(cls == level, kappa[level], kap)
        own_w = weight[:, slab]
        sub8 = lax.broadcasted_iota(jnp.int32, (8, LANES), 0)
        cells = []
        for r in range(RB):
            w_row = jnp.broadcast_to(own_w[r : r + 1], (8, LANES))
            k_row = jnp.broadcast_to(kap[r : r + 1], (8, LANES))
            cells.append(jnp.where(sub8 == 0, w_row, k_row))
        for q, part in enumerate(swap(cells)):
            PW[q] = part

        def shuffle_seen(i, c):
            lanes = pl.ds(pl.multiple_of(i * LANES, LANES), LANES)
            seen, rhs = [], []
            for r in range(RB):
                s = mask[r, :, lanes].astype(jnp.float32) * weight[r : r + 1, lanes]
                seen.append(s)
                rhs.append(s * obs[r, :, lanes])
            for q, part in enumerate(swap(rhs)):
                PR[4 * i + q] = part
            for q, part in enumerate(swap(seen)):
                PS[4 * i + q] = part
            return c

        lax.fori_loop(0, J // 4, shuffle_seen, 0)
        U[...] = jnp.zeros_like(U)

        pl.semaphore_wait(barrier, (J - 1) + (Z - 1) + 4)

        def cell_copy(q):
            return pltpu.make_async_remote_copy(
                src_ref=PW.at[q], dst_ref=CW.at[y], send_sem=cell_send.at[q],
                recv_sem=cell_recv.at[y], device_id=device(z, 4 * d + q), device_id_type=MESH,
            )

        def cell_local(q):
            return pltpu.make_async_copy(PW.at[q], CW.at[y], cell_recv.at[y])

        for q in range(4):
            @pl.when(4 * d + q != j)
            def _():
                cell_copy(q).start()

            @pl.when(4 * d + q == j)
            def _():
                cell_local(q).start()

        def to_tile(src, dst, at, i):
            jt = lax.rem(j + i, J)
            return pltpu.make_async_remote_copy(
                src_ref=src.at[jt], dst_ref=dst.at[y, pl.ds(pl.multiple_of(d * TB, TB), TB)],
                send_sem=all_send.at[at], recv_sem=all_recv.at[at],
                device_id=device(z, jt), device_id_type=MESH,
            )

        def to_days(src, dst, at, i):
            jt = lax.rem(j + i, J)
            yt, dt = place(jt)
            return pltpu.make_async_remote_copy(
                src_ref=src.at[yt, pl.ds(pl.multiple_of(dt * TB, TB), TB)], dst_ref=dst.at[j],
                send_sem=all_send.at[at], recv_sem=all_recv.at[at],
                device_id=device(z, jt), device_id_type=MESH,
            )

        def send_all(copy, src, dst, at):
            def one(i, c):
                copy(src, dst, at, i).start()
                return c

            lax.fori_loop(1, J, one, 0)

        def send_tile(src, dst, at):
            send_all(to_tile, src, dst, at)
            pltpu.make_async_copy(
                src.at[j], dst.at[y, pl.ds(pl.multiple_of(d * TB, TB), TB)], all_recv.at[at]
            ).start()

        def send_days(src, dst, at):
            send_all(to_days, src, dst, at)
            pltpu.make_async_copy(
                src.at[y, pl.ds(pl.multiple_of(d * TB, TB), TB)], dst.at[j], all_recv.at[at]
            ).start()

        def all_wait(dst, at):
            pltpu.make_async_copy(dst, dst, all_recv.at[at]).wait()

        def all_wait_send(at):
            pltpu.make_async_copy(
                PR.at[pl.ds(0, J - 1)], PR.at[pl.ds(0, J - 1)], all_send.at[at]
            ).wait()

        ways = []
        for dz, dj in ((-1, 0), (1, 0), (0, -1), (0, 1), (-1, -1), (-1, 1), (1, -1), (1, 1)):
            to_ok, from_ok = True, True
            if dz:
                to_ok, from_ok = (~top, ~bottom) if dz < 0 else (~bottom, ~top)
            if dj:
                a, b = (~left, ~right) if dj < 0 else (~right, ~left)
                to_ok, from_ok = (a, b) if to_ok is True else (to_ok & a, from_ok & b)
            zt = z if dz == 0 else (north if dz < 0 else south)
            jt = j if dj == 0 else (west if dj < 0 else east)
            ways.append((dz, dj, device(zt, jt), to_ok, from_ok))

        def near_copy(at):
            return pltpu.make_async_remote_copy(
                src_ref=CT, dst_ref=CN.at[at], send_sem=near_send.at[at],
                recv_sem=near_recv.at[at], device_id=ways[at][2], device_id_type=MESH,
            )

        def halo_copy(ge, n, w, at):
            dz, dj, target, _, _ = ways[at]
            def span(delta, size):
                if delta == 0:
                    return pl.ds(HALO, size), pl.ds(HALO, size)
                if delta < 0:
                    return pl.ds(HALO, HALO), pl.ds(HALO + size, HALO)
                return pl.ds(size, HALO), pl.ds(0, HALO)

            (rs, rd), (cs, cd) = span(dz, ROWS), span(dj, COLS)
            return pltpu.make_async_remote_copy(
                src_ref=ge.at[w, rs, cs], dst_ref=ge.at[w, rd, cd],
                send_sem=halo_send.at[n, w, at], recv_sem=halo_recv.at[n, w, at],
                device_id=target, device_id_type=MESH,
            )

        def each_way(which, do):
            for at, way in enumerate(ways):
                @pl.when(way[which])
                def _():
                    do(at)

        def halo_start(ge, n, w):
            each_way(3, lambda at: halo_copy(ge, n, w, at).start())

        def halo_wait(ge, n, w):
            each_way(4, lambda at: halo_copy(ge, n, w, at).wait_recv())

        send_tile(PR, XR, 0)

        for yt in range(Y):
            pltpu.make_async_copy(CW.at[yt], CW.at[yt], cell_recv.at[yt]).wait()
        packed = jnp.zeros((8, LANES), jnp.float32)
        for yt in range(Y):
            for f in range(2):
                packed = jnp.where(sub8 == Y * f + yt, CW[yt][f : f + 1], packed)
        CT[...] = packed
        each_way(3, lambda at: near_copy(at).start())

        column = lax.broadcasted_iota(jnp.int32, (8, LANES), 0) * K
        for k in range(K):
            outside = (left & (column + k < HALO)) | (right & (column + k >= HALO + COLS))
            MK[k] = jnp.where(outside, 0.0, 1.0)

        def spread_tile(source, dz, dj):
            for f, scale, shift in ((0, HALF_OBS, 0.0), (1, STENCIL_SCALE, 20.0)):
                for yt in range(Y):
                    if (dz < 0 and RB * (yt + 1) <= ROWS - HALO) or (dz > 0 and RB * yt >= HALO):
                        continue
                    at = Y * f + yt
                    flat = jnp.broadcast_to(source[at : at + 1], (LANES, LANES)) * scale + shift
                    turned = jnp.transpose(flat).reshape(RB, COLS, LANES)
                    row = HALO + dz * ROWS + RB * yt
                    if dj == 0:
                        NC[f, row : row + RB, OWN, :] = turned
                    elif dj < 0:
                        NC[f, row : row + RB, 0:HALO, :] = turned[:, COLS - HALO :]
                    else:
                        NC[f, row : row + RB, HALO + COLS : EC, :] = turned[:, :HALO]

        spread_tile(packed, 0, 0)
        each_way(4, lambda at: near_copy(at).wait_recv())
        for at, way in enumerate(ways):
            spread_tile(CN[at], -way[0], -way[1])

        def interleave_cells(e, c):
            for k in range(K):
                HC[e, k] = NC[0, e, pl.ds(k, 8, stride=K), :]
                KC[e, k] = NC[1, e, pl.ds(k, 8, stride=K), :]
            return c

        lax.fori_loop(0, ER, interleave_cells, 0)

        def dot(a, b, dims):
            return lax.dot_general(
                a, b, (dims, ((), ())), precision=lax.Precision.HIGHEST,
                preferred_element_type=jnp.float32,
            )

        def to_modes(tile, put):
            def one(i, c):
                v = jnp.concatenate([tile(2 * i), tile(2 * i + 1)], axis=1)
                h = dot(jnp.transpose(v), basis[...], ((1,), (0,)))
                for w in range(WIDE):
                    put(w, 2 * RB * i, h[:, w * LANES : (w + 1) * LANES].reshape(2 * RB, COLS, LANES))
                return c

            lax.fori_loop(0, Y // 2, one, 0)

        def to_time(get, out):
            def one(i, c):
                v = [get(w, pl.ds(2 * RB * i, 2 * RB)).reshape(2 * RB * COLS, LANES) for w in range(WIDE)]
                t = dot(basis[...], jnp.concatenate(v, axis=1), ((1,), (1,)))
                out[2 * i] = t[:, :LANES]
                out[2 * i + 1] = t[:, LANES:]
                return c

            lax.fori_loop(0, Y // 2, one, 0)

        def full(v):
            return jnp.broadcast_to(v, (8, LANES))

        def coefficients(w):
            lanes = slice(w * LANES, (w + 1) * LANES)
            return [modal[i : i + 1, lanes] for i in range(4)]

        def stencil(p, w, u):
            v = [U[p, w, u, k] for k in range(K)]
            s = [U[p, w, u - 1, k] + U[p, w, u + 1, k] for k in range(K)]
            a = [4.0 * v[k] + s[k] for k in range(K)]
            row = [pltpu.roll(a[K - 1], 1, 0)] + a + [pltpu.roll(a[0], 7, 0)]
            return v, [row[k] + row[k + 2] + 4.0 * s[k] for k in range(K)]

        def precondition(ge, w):
            eig6, inv_centre, stretch, inv_spread = coefficients(w)
            ic = full(inv_centre)

            def begin(i, c):
                for e in (2 * i, 2 * i + 1):
                    for k in range(K):
                        g = ge[w, e, pl.ds(k, 8, stride=K), :]
                        G[w, e, k] = g
                        U[0, w, e + 1, k] = g * ic
                return c

            lax.fori_loop(0, ER // 2, begin, 0)

            def sweep(n, ratio):
                p = n % 2
                ratio_next = 1.0 / (2.0 * stretch - ratio)
                momentum = ratio_next * ratio
                step = 2.0 * ratio_next * inv_spread
                cb, ce, c1 = full(step), full(step * eig6), full(1.0 + momentum)
                cp = full(jnp.where(n == 0, 0.0, momentum))
                clipped = (ER - HALO - n) // 2
                pairs = jnp.where(top | bottom, clipped, ER // 2 - 1 - n)
                low = jnp.where(top, HALO, jnp.where(bottom, ER - HALO - 2 * clipped, n + 1))

                def pair(i, c):
                    for e in (low + 2 * i, low + 2 * i + 1):
                        v, h = stencil(p, w, e + 1)
                        for k in range(K):
                            fresh = ce * (h[k] - KC[e, k] * v[k]) + cb * (G[w, e, k] - HC[e, k] * v[k])
                            fresh = fresh + (c1 * v[k] - cp * U[1 - p, w, e + 1, k])
                            U[1 - p, w, e + 1, k] = fresh * MK[k]
                    return c

                lax.fori_loop(0, pairs, pair, 0)
                return ratio_next

            lax.fori_loop(0, DEG - 1, sweep, 1.0 / stretch)

        def stencil_part(w, keep):
            eig6 = full(coefficients(w)[0])

            def one(i, c):
                for r in (2 * i, 2 * i + 1):
                    v, h = stencil((DEG - 1) % 2, w, r + HALO + 1)
                    for k in range(K):
                        keep[w, r, pl.ds(k, 8, stride=K), :] = v[k]
                        NQ[w, r, pl.ds(k, 8, stride=K), :] = eig6 * (KC[r + HALO, k] * v[k] - h[k])
                return c

            lax.fori_loop(0, ROWS // 2, one, 0)

        def pack(parts):
            out = jnp.zeros((8, LANES), jnp.float32)
            for at, part in enumerate(parts):
                out = jnp.where(sub8 == at, jnp.sum(part, axis=0, keepdims=True), out)
            return out

        def column_copy(at, i):
            return pltpu.make_async_remote_copy(
                src_ref=SA.at[at], dst_ref=RZ.at[at, z], send_sem=sum_send.at[at, 0],
                recv_sem=sum_recv.at[at, 0],
                device_id=(lax.rem(z + i, Z) * Y + y, d), device_id_type=MESH,
            )

        def plane_copy(at, i):
            return pltpu.make_async_remote_copy(
                src_ref=SG.at[at], dst_ref=RG.at[at, j], send_sem=sum_send.at[at, 1],
                recv_sem=sum_recv.at[at, 1],
                device_id=device(z, lax.rem(j + i, J)), device_id_type=MESH,
            )

        def wait_bytes(ref, count, sem):
            part = ref.at[pl.ds(0, count)]
            pltpu.make_async_copy(part, part, sem).wait()

        def column_start(at, value):
            SA[at] = value
            RZ[at, z] = value

            def one(i, c):
                column_copy(at, i).start()
                return c

            lax.fori_loop(1, Z, one, 0)

        def column_end(at):
            for side in (sum_recv, sum_send):
                wait_bytes(RZ.at[at], Z - 1, side.at[at, 0])
            return lax.fori_loop(1, Z, lambda i, c: c + RZ[at, i], RZ[at, 0])

        def plane_start(at, value):
            SG[at] = value
            RG[at, j] = value

            def one(i, c):
                plane_copy(at, i).start()
                return c

            lax.fori_loop(1, J, one, 0)

        def plane_end(at):
            for side in (sum_recv, sum_send):
                wait_bytes(RG.at[at], J - 1, side.at[at, 1])
            total = lax.fori_loop(1, J, lambda i, c: c + RG[at, i], RG[at, 0])
            return [jnp.sum(total[i : i + 1], axis=1, keepdims=True) for i in range(3)]

        zero = jnp.zeros((8, LANES), jnp.float32)

        def fold_cells(v):
            return jnp.sum(v.reshape(COLS // 8, 8, LANES), axis=0)

        def put_first(w, row, v):
            GE1[w, pl.ds(HALO + row, 2 * RB), OWN, :] = v

        def put_seen(w, row, v):
            NAT[w, pl.ds(row, 2 * RB)] = v

        all_wait(XR, 0)
        to_modes(lambda i: XR[i], put_first)
        for w in range(WIDE):
            halo_start(GE1, 0, w)
        send_tile(PS, XS, 1)
        for w in range(WIDE):
            halo_wait(GE1, 0, w)
            precondition(GE1, w)
            stencil_part(w, NZ)
        to_time(lambda w, rows: NZ[w, rows, OWN, :], TZ)
        all_wait(XS, 1)
        to_modes(lambda i: TZ[i] * XS[i], put_seen)

        sums = (zero, zero)
        for w in range(WIDE):
            def first_image(r, acc):
                fit, curve = acc
                zh = NZ[w, r, OWN, :]
                q = NQ[w, r, OWN, :] + NAT[w, r]
                GE2[w, r + HALO, OWN, :] = q
                return fit + fold_cells(GE1[w, r + HALO, OWN, :] * zh), curve + fold_cells(zh * q)

            sums = lax.fori_loop(0, ROWS, first_image, sums)
            halo_start(GE2, 1, w)
        column_start(0, pack(sums))
        send_days(TZ, FZ, 2)
        to_time(lambda w, rows: GE2[w, pl.ds(rows.start + HALO, rows.size), OWN, :], TQ)
        send_days(TQ, FQ, 3)

        for w in range(WIDE):
            halo_wait(GE2, 1, w)
            precondition(GE2, w)
            stencil_part(w, NW)
            if w == 0:
                plane_start(0, column_end(0))
        to_time(lambda w, rows: NW[w, rows, OWN, :], TW)
        send_days(TW, FW, 4)
        to_modes(lambda i: TW[i] * XS[i], put_seen)
        fit0, curve0, _ = plane_end(0)
        alpha0 = fit0 / curve0

        sums = (zero, zero, zero)
        for w in range(WIDE):
            def second_image(r, acc):
                fit, curve, cross = acc
                wh, g = NW[w, r, OWN, :], GE2[w, r + HALO, OWN, :]
                q = NQ[w, r, OWN, :] + NAT[w, r]
                NV[w, r] = q
                z1 = NZ[w, r, OWN, :] - alpha0 * wh
                r1 = GE1[w, r + HALO, OWN, :] - alpha0 * g
                return (
                    fit + fold_cells(r1 * z1), curve + fold_cells(z1 * (g - alpha0 * q)),
                    cross + fold_cells(z1 * g),
                )

            sums = lax.fori_loop(0, ROWS, second_image, sums)
        column_start(1, pack(sums))
        to_time(lambda w, rows: NV[w, rows], TV)
        send_days(TV, FV, 5)
        plane_start(1, column_end(1))
        fit1, curve1, cross1 = plane_end(1)
        beta = fit1 / fit0
        alpha1 = fit1 / (curve1 + 2.0 * beta * cross1 + beta * beta * curve0)
        c_old = alpha0 + alpha1 + alpha1 * beta
        c_new = alpha0 * alpha1

        def finish(part):
            def one(i, c):
                lanes = pl.ds(pl.multiple_of(i * LANES, LANES), LANES)
                values = []
                for q in range(4):
                    at = 4 * i + q
                    if part == 0:
                        values.append(c_old * FZ[at] - c_new * FW[at])
                    else:
                        values.append(PR[at] - c_old * FQ[at] + c_new * FV[at])
                for r, v in enumerate(swap(values)):
                    (sol, res)[part][r, :, lanes] = v
                return c

            lax.fori_loop(0, J // 4, one, 0)

        all_wait(FZ, 2)
        all_wait(FQ, 3)
        all_wait(FW, 4)
        finish(0)
        all_wait(FV, 5)
        finish(1)

        for at in range(6):
            all_wait_send(at)
        for q in range(4):
            @pl.when(4 * d + q != j)
            def _():
                cell_copy(q).wait_send()
        each_way(3, lambda at: near_copy(at).wait_send())
        for n, ge in enumerate((GE1, GE2)):
            for w in range(WIDE):
                each_way(3, lambda at: halo_copy(ge, n, w, at).wait_send())

    f32 = jnp.float32
    extended = pltpu.VMEM((WIDE, ER, EC, LANES), f32)
    strip = pltpu.VMEM((WIDE, ROWS, EC, LANES), f32)
    flat = pltpu.VMEM((WIDE, ROWS, COLS, LANES), f32)
    cell = pltpu.VMEM((ER, K, 8, LANES), f32)
    days = pltpu.VMEM((J, TB, LANES), f32)
    tile = pltpu.VMEM((Y, NT, LANES), f32)
    dma = pltpu.SemaphoreType.DMA
    scratch = [
        extended, extended, pltpu.VMEM((2, WIDE, ER + 2, K, 8, LANES), f32),
        pltpu.VMEM((WIDE, ER, K, 8, LANES), f32), cell, cell, pltpu.VMEM((2, ER, EC, LANES), f32),
        pltpu.VMEM((K, 8, LANES), f32), flat, strip, strip, strip, flat, days, days, tile, tile,
        tile, tile, tile, tile, days, days, days, days,
        pltpu.VMEM((4, 8, LANES), f32), pltpu.VMEM((Y, 8, LANES), f32),
        pltpu.VMEM((8, LANES), f32), pltpu.VMEM((8, 8, LANES), f32),
        pltpu.VMEM((2, 8, LANES), f32), pltpu.VMEM((2, Z, 8, LANES), f32),
        pltpu.VMEM((2, 8, LANES), f32), pltpu.VMEM((2, J, 8, LANES), f32),
        dma((2, WIDE, 8)), dma((2, WIDE, 8)), dma((8,)), dma((8,)), dma((6,)), dma((6,)),
        dma((4,)), dma((Y,)), dma((2, 2)), dma((2, 2)),
    ]
    return kernel, scratch


def solution(mesh):
    Z = mesh.shape["rows"] // Y
    D = mesh.shape["days"]
    kernel, scratch = make_kernel(Z, D)
    basis, modal = modal_constants(TB * D)
    vmem = pl.BlockSpec(memory_space=pltpu.VMEM)
    smem = pl.BlockSpec(memory_space=pltpu.SMEM)

    def body(observations, obs_mask, obs_weight, classes, kappa_table):
        shape = jax.ShapeDtypeStruct((RB, TB, COLS * Y * D), jnp.float32)
        sol, res = pl.pallas_call(
            kernel,
            out_shape=(shape, shape),
            in_specs=[vmem] * 4 + [smem] + [vmem] * 2,
            out_specs=(vmem, vmem),
            scratch_shapes=scratch,
            compiler_params=pltpu.CompilerParams(
                collective_id=0, has_side_effects=True, vmem_limit_bytes=48 * 1024 * 1024
            ),
        )(
            jnp.transpose(observations, (1, 0, 2)), jnp.transpose(obs_mask, (1, 0, 2)),
            obs_weight, classes, kappa_table, jnp.asarray(basis), jnp.asarray(modal),
        )
        return jnp.transpose(sol, (1, 0, 2)), jnp.transpose(res, (1, 0, 2))

    in_specs = (P("days", "rows", None), P("days", "rows", None), P("rows", None), P("rows", None), P())
    out_specs = (P("days", "rows", None), P("days", "rows", None))
    return jax.shard_map(body, mesh=mesh, in_specs=in_specs, out_specs=out_specs, check_vma=False)
```

```python
import math

import jax
import jax.numpy as jnp
import numpy as np
from jax import lax
from jax.experimental import pallas as pl
from jax.experimental.pallas import tpu as pltpu
from jax.sharding import PartitionSpec as P

MESH = pl.DeviceIdType.MESH
DEG = 8
TIME_SHIFT = 0.05
HALF_OBS = 0.5
KAPPA_LOW = 0.02
KAPPA_HIGH = 2.0
WEIGHT_LOW = 0.5
WEIGHT_HIGH = 4.0
STENCIL_SCALE = 6.0
STENCIL_TOP = 16.0 / 3.0

Y = 4
TB = 32
RB = 4
COLS = 32
HALO = 8
K = (COLS + 2 * HALO) // 8
LANES = 128
GROUP = 4


def modal_constants(total):
    order = np.arange(1, total + 1, dtype=np.float64)
    phase = np.outer(order, order) % (2 * (total + 1))
    basis = np.sqrt(2.0 / (total + 1)) * np.sin(np.pi * phase / (total + 1))
    eig = 2.0 + TIME_SHIFT - 2.0 * np.cos(np.pi * order / (total + 1))
    lower = eig * KAPPA_LOW + HALF_OBS * WEIGHT_LOW
    upper = eig * (KAPPA_HIGH + STENCIL_TOP) + HALF_OBS * WEIGHT_HIGH
    centre, spread = 0.5 * (upper + lower), 0.5 * (upper - lower)
    rows = np.zeros((8, total), np.float32)
    for at, row in enumerate(
        (eig / STENCIL_SCALE, 1.0 / centre, centre / spread, 1.0 / spread, STENCIL_SCALE / eig)
    ):
        rows[at] = row
    return basis.astype(np.float32), rows


def make_kernel(Z, D):
    NT = TB * D
    ROWS = RB * Y
    J = Y * D
    WIDE = NT // LANES
    DBITS = D.bit_length() - 1
    SLABS = J // 4
    ER, EC = ROWS + 2 * HALO, COLS + 2 * HALO
    OWN = pl.ds(HALO, COLS)

    def kernel(
        obs_in, mask_in, weight_in, classes_in, kappa, basis_in, modal_in, sol, res,
        obs, mask, weight, classes, basis, modal,
        GE1, GE2, U, DX, G, KC, SC, NC, MK, NAT, NQ, NZ, NW, NV, PR, PS, XR, XS,
        TZ, TQ, TW, TV, FZ, FQ, FW, FV, PW, CW, CT, CN, SA, RZ, SG, RG,
        halo_send, halo_recv, near_send, near_recv, all_send, all_recv, cell_send, cell_recv,
        sum_send, sum_recv, load_sem,
    ):
        ri, d = lax.axis_index("rows"), lax.axis_index("days")
        z, y = ri // Y, ri % Y
        j = y * D + (d ^ ((D - 1) * (y & 1)))
        top, bottom, left, right = z == 0, z == Z - 1, j == 0, j == J - 1

        def place(jt):
            yt = jt >> DBITS
            return yt, (jt & (D - 1)) ^ ((D - 1) * (yt & 1))

        def device(zt, jt):
            yt, dt = place(jt)
            return (zt * Y + yt, dt)

        north, south = lax.rem(z + Z - 1, Z), lax.rem(z + 1, Z)
        west, east = lax.rem(j + J - 1, J), lax.rem(j + 1, J)

        CN[...] = jnp.zeros_like(CN)
        loads = [
            pltpu.make_async_copy(src, dst, load_sem.at[i])
            for i, (src, dst) in enumerate((
                (weight_in, weight), (classes_in, classes), (obs_in, obs), (mask_in, mask),
                (basis_in, basis), (modal_in, modal),
            ))
        ]
        for load in loads:
            load.start()

        barrier = pltpu.get_barrier_semaphore()

        def greet(target):
            pl.semaphore_signal(barrier, inc=1, device_id=target, device_id_type=MESH)

        def greet_plane(i, c):
            greet(device(z, ((j + i) & (J - 1))))
            return c

        def greet_column(i, c):
            greet((((z + i) & (Z - 1)) * Y + y, d))
            return c

        lax.fori_loop(1, J, greet_plane, 0)
        lax.fori_loop(1, Z, greet_column, 0)
        for zt in (north, south):
            for jt in (west, east):
                greet(device(zt, jt))

        def full(v):
            return jnp.broadcast_to(v, (8, LANES))

        def swap(parts):
            lane = lax.broadcasted_iota(jnp.int32, parts[0].shape, 1)
            wide, even = lane < 64, (lane // 32) % 2 == 0
            t0 = jnp.where(wide, parts[0], pltpu.roll(parts[2], 64, 1))
            t2 = jnp.where(wide, pltpu.roll(parts[0], 64, 1), parts[2])
            t1 = jnp.where(wide, parts[1], pltpu.roll(parts[3], 64, 1))
            t3 = jnp.where(wide, pltpu.roll(parts[1], 64, 1), parts[3])
            d0 = jnp.where(even, t0, pltpu.roll(t1, 32, 1))
            d1 = jnp.where(even, pltpu.roll(t0, 96, 1), t1)
            d2 = jnp.where(even, t2, pltpu.roll(t3, 32, 1))
            d3 = jnp.where(even, pltpu.roll(t2, 96, 1), t3)
            return d0, d1, d2, d3

        loads[0].wait()
        loads[1].wait()
        slab = pl.ds(pl.multiple_of(d * LANES, LANES), LANES)
        cls = classes[:, slab]
        kap = jnp.zeros((RB, LANES), jnp.float32)
        for level in range(16):
            kap = jnp.where(cls == level, kappa[level], kap)
        own_w = weight[:, slab]
        sub8 = lax.broadcasted_iota(jnp.int32, (8, LANES), 0)
        cells = []
        for r in range(RB):
            w_row = jnp.broadcast_to(own_w[r : r + 1], (8, LANES))
            k_row = jnp.broadcast_to(kap[r : r + 1], (8, LANES))
            cells.append(jnp.where(sub8 == 0, w_row, k_row))
        for q, part in enumerate(swap(cells)):
            PW[q] = part

        pl.semaphore_wait(barrier, (J - 1) + (Z - 1) + 4)

        def cell_copy(q):
            return pltpu.make_async_remote_copy(
                src_ref=PW.at[q], dst_ref=CW.at[y], send_sem=cell_send.at[q],
                recv_sem=cell_recv.at[y], device_id=device(z, 4 * d + q), device_id_type=MESH,
            )

        def cell_local(q):
            return pltpu.make_async_copy(PW.at[q], CW.at[y], cell_recv.at[y])

        for q in range(4):
            @pl.when(4 * d + q != j)
            def _():
                cell_copy(q).start()

            @pl.when(4 * d + q == j)
            def _():
                cell_local(q).start()

        def to_tile(src, dst, at, i):
            jt = ((j + i) & (J - 1))
            return pltpu.make_async_remote_copy(
                src_ref=src.at[jt], dst_ref=dst.at[y, pl.ds(pl.multiple_of(d * TB, TB), TB)],
                send_sem=all_send.at[at], recv_sem=all_recv.at[at],
                device_id=device(z, jt), device_id_type=MESH,
            )

        def to_days(src, dst, at, i):
            jt = ((j + i) & (J - 1))
            yt, dt = place(jt)
            return pltpu.make_async_remote_copy(
                src_ref=src.at[yt, pl.ds(pl.multiple_of(dt * TB, TB), TB)], dst_ref=dst.at[j],
                send_sem=all_send.at[at], recv_sem=all_recv.at[at],
                device_id=device(z, jt), device_id_type=MESH,
            )

        def send_range(copy, src, dst, at, low, high):
            def one(i, c):
                copy(src, dst, at, i).start()
                return c

            lax.fori_loop(low, high, one, 0)

        def own_tile(src, dst, at):
            pltpu.make_async_copy(
                src.at[j], dst.at[y, pl.ds(pl.multiple_of(d * TB, TB), TB)], all_recv.at[at]
            ).start()

        def own_days(src, dst, at):
            pltpu.make_async_copy(
                src.at[y, pl.ds(pl.multiple_of(d * TB, TB), TB)], dst.at[j], all_recv.at[at]
            ).start()

        def send_tile(src, dst, at):
            send_range(to_tile, src, dst, at, 1, J)
            own_tile(src, dst, at)

        def send_days(src, dst, at):
            send_range(to_days, src, dst, at, 1, J)
            own_days(src, dst, at)

        def all_wait(dst, at):
            pltpu.make_async_copy(dst, dst, all_recv.at[at]).wait()

        def all_wait_send(at):
            pltpu.make_async_copy(
                PR.at[pl.ds(0, J - 1)], PR.at[pl.ds(0, J - 1)], all_send.at[at]
            ).wait()

        ways = []
        for dz, dj in ((-1, 0), (1, 0), (0, -1), (0, 1), (-1, -1), (-1, 1), (1, -1), (1, 1)):
            to_ok, from_ok = True, True
            if dz:
                to_ok, from_ok = (~top, ~bottom) if dz < 0 else (~bottom, ~top)
            if dj:
                a, b = (~left, ~right) if dj < 0 else (~right, ~left)
                to_ok, from_ok = (a, b) if to_ok is True else (to_ok & a, from_ok & b)
            zt = z if dz == 0 else (north if dz < 0 else south)
            jt = j if dj == 0 else (west if dj < 0 else east)
            ways.append((dz, dj, device(zt, jt), to_ok, from_ok))

        def near_copy(at):
            return pltpu.make_async_remote_copy(
                src_ref=CT, dst_ref=CN.at[at], send_sem=near_send.at[at],
                recv_sem=near_recv.at[at], device_id=ways[at][2], device_id_type=MESH,
            )

        def halo_copy(ge, n, w, at):
            dz, dj, target, _, _ = ways[at]
            def span(delta, size):
                if delta == 0:
                    return pl.ds(HALO, size), pl.ds(HALO, size)
                if delta < 0:
                    return pl.ds(HALO, HALO), pl.ds(HALO + size, HALO)
                return pl.ds(size, HALO), pl.ds(0, HALO)

            (rs, rd), (cs, cd) = span(dz, ROWS), span(dj, COLS)
            return pltpu.make_async_remote_copy(
                src_ref=ge.at[w, rs, cs], dst_ref=ge.at[w, rd, cd],
                send_sem=halo_send.at[n, w, at], recv_sem=halo_recv.at[n, w, at],
                device_id=target, device_id_type=MESH,
            )

        def each_way(which, do):
            for at, way in enumerate(ways):
                @pl.when(way[which])
                def _():
                    do(at)

        def halo_start(ge, n, w):
            each_way(3, lambda at: halo_copy(ge, n, w, at).start())

        def halo_wait(ge, n, w):
            each_way(4, lambda at: halo_copy(ge, n, w, at).wait_recv())

        def day_rows(i, r, t):
            return pl.ds(t * SLABS * RB + RB * i + r, 8, stride=SLABS * RB)

        def seen_rows(i, r):
            lanes = pl.ds(pl.multiple_of(i * LANES, LANES), LANES)
            seen = [mask[day_rows(i, r, t), :] for t in range(0, TB, 8)]
            return jnp.concatenate(seen, axis=0).astype(jnp.float32) * weight[r : r + 1, lanes]

        for load in loads[2:]:
            load.wait()

        def shuffle_rhs(step, c):
            i = ((j >> 2) + step) & (SLABS - 1)
            rhs = []
            for r in range(RB):
                seen = [obs[day_rows(i, r, t), :] for t in range(0, TB, 8)]
                rhs.append(seen_rows(i, r) * jnp.concatenate(seen, axis=0))
            for q, part in enumerate(swap(rhs)):
                PR[4 * i + q] = part
            for q in range(4):
                @pl.when(4 * i + q != j)
                def _():
                    to_tile(PR, XR, 0, 4 * i + q - j).start()

            return c

        lax.fori_loop(0, SLABS, shuffle_rhs, 0)
        own_tile(PR, XR, 0)

        def shuffle_seen(i, c):
            for q, part in enumerate(swap([seen_rows(i, r) for r in range(RB)])):
                PS[4 * i + q] = part
            return c

        lax.fori_loop(0, SLABS, shuffle_seen, 0)

        for cond, rows, cols in (
            (top, pl.ds(0, HALO), pl.ds(0, EC)),
            (bottom, pl.ds(HALO + ROWS, HALO), pl.ds(0, EC)),
            (left, pl.ds(0, ER), pl.ds(0, HALO)),
            (right, pl.ds(0, ER), pl.ds(HALO + COLS, HALO)),
        ):
            @pl.when(cond)
            def _():
                for ge in (GE1, GE2):
                    for w in range(WIDE):
                        ge[w, rows, cols, :] = jnp.zeros((rows.size, cols.size, LANES), jnp.float32)

        U[...] = jnp.zeros_like(U)

        for yt in range(Y):
            pltpu.make_async_copy(CW.at[yt], CW.at[yt], cell_recv.at[yt]).wait()
        packed = jnp.zeros((8, LANES), jnp.float32)
        for yt in range(Y):
            for f in range(2):
                packed = jnp.where(sub8 == Y * f + yt, CW[yt][f : f + 1], packed)
        CT[...] = packed
        each_way(3, lambda at: near_copy(at).start())

        column = lax.broadcasted_iota(jnp.int32, (8, LANES), 0) * K
        for k in range(K):
            outside = (left & (column + k < HALO)) | (right & (column + k >= HALO + COLS))
            MK[k] = jnp.where(outside, 0.0, 1.0)

        def spread_tile(source, dz, dj):
            for f, scale, shift in ((0, HALF_OBS, 0.0), (1, STENCIL_SCALE, 36.0)):
                for yt in range(Y):
                    if (dz < 0 and RB * (yt + 1) <= ROWS - HALO) or (dz > 0 and RB * yt >= HALO):
                        continue
                    at = Y * f + yt
                    flat = jnp.broadcast_to(source[at : at + 1], (LANES, LANES)) * scale + shift
                    turned = jnp.transpose(flat).reshape(RB, COLS, LANES)
                    row = HALO + dz * ROWS + RB * yt
                    if dj == 0:
                        NC[f, row : row + RB, OWN, :] = turned
                    elif dj < 0:
                        NC[f, row : row + RB, 0:HALO, :] = turned[:, COLS - HALO :]
                    else:
                        NC[f, row : row + RB, HALO + COLS : EC, :] = turned[:, :HALO]

        spread_tile(packed, 0, 0)
        each_way(4, lambda at: near_copy(at).wait_recv())
        for at, way in enumerate(ways):
            spread_tile(CN[at], -way[0], -way[1])

        inv_eig = [full(modal[4:5, w * LANES : (w + 1) * LANES]) for w in range(WIDE)]

        def interleave_cells(e, c):
            for k in range(K):
                hc = NC[0, e, pl.ds(k, 8, stride=K), :]
                kc = NC[1, e, pl.ds(k, 8, stride=K), :]
                KC[e, k] = kc
                for w in range(WIDE):
                    SC[w, e, k] = hc * inv_eig[w] + kc
            return c

        lax.fori_loop(0, ER, interleave_cells, 0)

        def dot(a, b, dims):
            return lax.dot_general(
                a, b, (dims, ((), ())), precision=lax.Precision.HIGHEST,
                preferred_element_type=jnp.float32,
            )

        def to_modes(tile, put):
            def one(i, c):
                v = jnp.concatenate([tile(2 * i), tile(2 * i + 1)], axis=1)
                h = dot(jnp.transpose(v), basis[...], ((1,), (0,)))
                for w in range(WIDE):
                    put(w, 2 * RB * i, h[:, w * LANES : (w + 1) * LANES].reshape(2 * RB, COLS, LANES))
                return c

            lax.fori_loop(0, Y // 2, one, 0)

        def to_time(get, out):
            def one(i, c):
                v = [get(w, pl.ds(2 * RB * i, 2 * RB)).reshape(2 * RB * COLS, LANES) for w in range(WIDE)]
                t = dot(basis[...], jnp.concatenate(v, axis=1), ((1,), (1,)))
                out[2 * i] = t[:, :LANES]
                out[2 * i + 1] = t[:, LANES:]
                return c

            lax.fori_loop(0, Y // 2, one, 0)

        def coefficients(w):
            lanes = slice(w * LANES, (w + 1) * LANES)
            return [modal[i : i + 1, lanes] for i in range(4)]

        def rows_of(p, w, first, count):
            above = [U[p, w, first, k] for k in range(K)]
            here = [U[p, w, first + 1, k] for k in range(K)]
            for i in range(count):
                below = [U[p, w, first + 2 + i, k] for k in range(K)]
                b = [4.0 * here[k] + (above[k] + below[k]) for k in range(K)]
                line = [pltpu.roll(b[K - 1], 1, 0)] + b + [pltpu.roll(b[0], 7, 0)]
                yield i, here, [(line[k] + line[k + 2]) + 4.0 * b[k] for k in range(K)]
                above, here = here, below

        def precondition(ge, w):
            eig6, inv_centre, stretch, inv_spread = coefficients(w)
            ic, ie = full(inv_centre), inv_eig[w]

            def begin(i, c):
                for e in (2 * i, 2 * i + 1):
                    for k in range(K):
                        g = ge[w, e, pl.ds(k, 8, stride=K), :]
                        G[w, e, k] = g * ie
                        u = g * ic
                        U[0, w, e + 1, k] = u
                        DX[w, e, k] = u
                return c

            lax.fori_loop(0, ER // 2, begin, 0)

            def sweep(n, ratio):
                p = n % 2
                ratio_next = 1.0 / (2.0 * stretch - ratio)
                momentum = full(ratio_next * ratio)
                step = full(2.0 * ratio_next * inv_spread * eig6)
                clipped = (ER - HALO + GROUP - 2 - n) // GROUP
                groups = jnp.where(top | bottom, clipped, (ER + GROUP - 3 - 2 * n) // GROUP)
                low = jnp.where(bottom, ER - HALO - GROUP * groups, ER // 2 - GROUP // 2 * groups)
                low = jnp.where(top, HALO, low)

                def group(i, c):
                    first = low + GROUP * i
                    for at, v, h in rows_of(p, w, first, GROUP):
                        e = first + at
                        for k in range(K):
                            dx = step * ((G[w, e, k] - SC[w, e, k] * v[k]) + h[k])
                            dx = (momentum * DX[w, e, k] + dx) * MK[k]
                            DX[w, e, k] = dx
                            U[1 - p, w, e + 1, k] = v[k] + dx
                    return c

                lax.fori_loop(0, groups, group, 0)
                return ratio_next

            lax.fori_loop(0, DEG - 1, sweep, 1.0 / stretch)

        def stencil_part(w, keep):
            eig6 = full(coefficients(w)[0])

            def one(i, c):
                first = GROUP * i
                for at, v, h in rows_of((DEG - 1) % 2, w, first + HALO, GROUP):
                    r = first + at
                    for k in range(K):
                        keep[w, r, pl.ds(k, 8, stride=K), :] = v[k]
                        NQ[w, r, pl.ds(k, 8, stride=K), :] = eig6 * (KC[r + HALO, k] * v[k] - h[k])
                return c

            lax.fori_loop(0, ROWS // GROUP, one, 0)

        def pack(parts):
            out = jnp.zeros((8, LANES), jnp.float32)
            for at, part in enumerate(parts):
                out = jnp.where(sub8 == at, jnp.sum(part, axis=0, keepdims=True), out)
            return out

        def column_copy(at, i):
            return pltpu.make_async_remote_copy(
                src_ref=SA.at[at], dst_ref=RZ.at[at, z], send_sem=sum_send.at[at, 0],
                recv_sem=sum_recv.at[at, 0],
                device_id=(((z + i) & (Z - 1)) * Y + y, d), device_id_type=MESH,
            )

        def plane_copy(at, i):
            return pltpu.make_async_remote_copy(
                src_ref=SG.at[at], dst_ref=RG.at[at, j], send_sem=sum_send.at[at, 1],
                recv_sem=sum_recv.at[at, 1],
                device_id=device(z, ((j + i) & (J - 1))), device_id_type=MESH,
            )

        def wait_bytes(ref, count, sem):
            part = ref.at[pl.ds(0, count)]
            pltpu.make_async_copy(part, part, sem).wait()

        def column_start(at, value):
            SA[at] = value
            RZ[at, z] = value

            def one(i, c):
                column_copy(at, i).start()
                return c

            lax.fori_loop(1, Z, one, 0)

        def column_end(at):
            for side in (sum_recv, sum_send):
                wait_bytes(RZ.at[at], Z - 1, side.at[at, 0])
            return lax.fori_loop(1, Z, lambda i, c: c + RZ[at, i], RZ[at, 0])

        def plane_start(at, value):
            SG[at] = value
            RG[at, j] = value

            def one(i, c):
                plane_copy(at, i).start()
                return c

            lax.fori_loop(1, J, one, 0)

        def plane_end(at):
            for side in (sum_recv, sum_send):
                wait_bytes(RG.at[at], J - 1, side.at[at, 1])
            total = lax.fori_loop(1, J, lambda i, c: c + RG[at, i], RG[at, 0])
            return [jnp.sum(total[i : i + 1], axis=1, keepdims=True) for i in range(3)]

        zero = jnp.zeros((8, LANES), jnp.float32)

        def fold_cells(v):
            return jnp.sum(v.reshape(COLS // 8, 8, LANES), axis=0)

        def put_first(w, row, v):
            GE1[w, pl.ds(HALO + row, 2 * RB), OWN, :] = v

        def put_seen(w, row, v):
            NAT[w, pl.ds(row, 2 * RB)] = v

        all_wait(XR, 0)
        to_modes(lambda i: XR[i], put_first)
        for w in range(WIDE):
            halo_start(GE1, 0, w)
        send_tile(PS, XS, 1)
        for w in range(WIDE):
            halo_wait(GE1, 0, w)
            precondition(GE1, w)
            stencil_part(w, NZ)
        to_time(lambda w, rows: NZ[w, rows, OWN, :], TZ)
        all_wait(XS, 1)
        to_modes(lambda i: TZ[i] * XS[i], put_seen)

        sums = (zero, zero)
        for w in range(WIDE):
            def first_image(r, acc):
                fit, curve = acc
                zh = NZ[w, r, OWN, :]
                q = NQ[w, r, OWN, :] + NAT[w, r]
                GE2[w, r + HALO, OWN, :] = q
                return fit + fold_cells(GE1[w, r + HALO, OWN, :] * zh), curve + fold_cells(zh * q)

            sums = lax.fori_loop(0, ROWS, first_image, sums)
            halo_start(GE2, 1, w)
        column_start(0, pack(sums))
        send_days(TZ, FZ, 2)
        to_time(lambda w, rows: GE2[w, pl.ds(rows.start + HALO, rows.size), OWN, :], TQ)
        send_days(TQ, FQ, 3)

        for w in range(WIDE):
            halo_wait(GE2, 1, w)
            precondition(GE2, w)
            stencil_part(w, NW)
            if w == 0:
                plane_start(0, column_end(0))
        to_time(lambda w, rows: NW[w, rows, OWN, :], TW)
        send_days(TW, FW, 4)
        to_modes(lambda i: TW[i] * XS[i], put_seen)
        fit0, curve0, _ = plane_end(0)
        alpha0 = fit0 / curve0

        sums = (zero, zero, zero)
        for w in range(WIDE):
            def second_image(r, acc):
                fit, curve, cross = acc
                wh, g = NW[w, r, OWN, :], GE2[w, r + HALO, OWN, :]
                q = NQ[w, r, OWN, :] + NAT[w, r]
                NV[w, r] = q
                z1 = NZ[w, r, OWN, :] - alpha0 * wh
                r1 = GE1[w, r + HALO, OWN, :] - alpha0 * g
                return (
                    fit + fold_cells(r1 * z1), curve + fold_cells(z1 * (g - alpha0 * q)),
                    cross + fold_cells(z1 * g),
                )

            sums = lax.fori_loop(0, ROWS, second_image, sums)
        column_start(1, pack(sums))
        to_time(lambda w, rows: NV[w, rows], TV)
        own_days(TV, FV, 5)
        send_range(to_days, TV, FV, 5, 1, 12)
        plane_start(1, column_end(1))
        send_range(to_days, TV, FV, 5, 12, J)
        fit1, curve1, cross1 = plane_end(1)
        beta = fit1 / fit0
        alpha1 = fit1 / (curve1 + 2.0 * beta * cross1 + beta * beta * curve0)
        c_old = alpha0 + alpha1 + alpha1 * beta
        c_new = alpha0 * alpha1

        def finish(part):
            def one(i, c):
                values = []
                for q in range(4):
                    at = 4 * i + q
                    if part == 0:
                        values.append(c_old * FZ[at] - c_new * FW[at])
                    else:
                        values.append(PR[at] - c_old * FQ[at] + c_new * FV[at])
                for r, v in enumerate(swap(values)):
                    for t in range(0, TB, 8):
                        (sol, res)[part][day_rows(i, r, t), :] = v[t : t + 8]
                return c

            lax.fori_loop(0, SLABS, one, 0)

        all_wait(FZ, 2)
        all_wait(FW, 4)
        finish(0)
        all_wait(FQ, 3)
        all_wait(FV, 5)
        finish(1)

        for at in range(6):
            all_wait_send(at)
        for q in range(4):
            @pl.when(4 * d + q != j)
            def _():
                cell_copy(q).wait_send()
        each_way(3, lambda at: near_copy(at).wait_send())
        for n, ge in enumerate((GE1, GE2)):
            for w in range(WIDE):
                each_way(3, lambda at: halo_copy(ge, n, w, at).wait_send())

    f32 = jnp.float32
    extended = pltpu.VMEM((WIDE, ER, EC, LANES), f32)
    strip = pltpu.VMEM((WIDE, ROWS, EC, LANES), f32)
    flat = pltpu.VMEM((WIDE, ROWS, COLS, LANES), f32)
    fields = pltpu.VMEM((WIDE, ER, K, 8, LANES), f32)
    cell = pltpu.VMEM((ER, K, 8, LANES), f32)
    days = pltpu.VMEM((J, TB, LANES), f32)
    tile = pltpu.VMEM((Y, NT, LANES), f32)
    dma = pltpu.SemaphoreType.DMA
    given = pltpu.VMEM((TB * SLABS * RB, LANES), f32)
    scratch = [
        given, pltpu.VMEM((TB * SLABS * RB, LANES), jnp.int32), pltpu.VMEM((RB, J * COLS), f32),
        pltpu.VMEM((RB, J * COLS), jnp.int32), pltpu.VMEM((NT, NT), f32), pltpu.VMEM((8, NT), f32),
        extended, extended, pltpu.VMEM((2, WIDE, ER + 2, K, 8, LANES), f32),
        fields, fields, cell, fields, pltpu.VMEM((2, ER, EC, LANES), f32),
        pltpu.VMEM((K, 8, LANES), f32), flat, strip, strip, strip, flat, days, days, tile, tile,
        tile, tile, tile, tile, days, days, days, days,
        pltpu.VMEM((4, 8, LANES), f32), pltpu.VMEM((Y, 8, LANES), f32),
        pltpu.VMEM((8, LANES), f32), pltpu.VMEM((8, 8, LANES), f32),
        pltpu.VMEM((2, 8, LANES), f32), pltpu.VMEM((2, Z, 8, LANES), f32),
        pltpu.VMEM((2, 8, LANES), f32), pltpu.VMEM((2, J, 8, LANES), f32),
        dma((2, WIDE, 8)), dma((2, WIDE, 8)), dma((8,)), dma((8,)), dma((6,)), dma((6,)),
        dma((4,)), dma((Y,)), dma((2, 2)), dma((2, 2)), dma((6,)),
    ]
    return kernel, scratch


def solution(mesh):
    Z = mesh.shape["rows"] // Y
    D = mesh.shape["days"]
    kernel, scratch = make_kernel(Z, D)
    basis, modal = modal_constants(TB * D)
    slabs = Y * D // 4
    vmem = pl.BlockSpec(memory_space=pltpu.VMEM)
    smem = pl.BlockSpec(memory_space=pltpu.SMEM)
    hbm = pl.BlockSpec(memory_space=pl.ANY)

    def by_slab(array):
        array = array.reshape(TB, RB, slabs, LANES)
        return jnp.transpose(array, (0, 2, 1, 3)).reshape(TB * slabs * RB, LANES)

    def by_row(array):
        array = array.reshape(TB, slabs, RB, LANES)
        return jnp.transpose(array, (0, 2, 1, 3)).reshape(TB, RB, slabs * LANES)

    def body(observations, obs_mask, obs_weight, classes, kappa_table):
        shape = jax.ShapeDtypeStruct((TB * slabs * RB, LANES), jnp.float32)
        sol, res = pl.pallas_call(
            kernel,
            out_shape=(shape, shape),
            in_specs=[hbm] * 4 + [smem] + [hbm] * 2,
            out_specs=(vmem, vmem),
            scratch_shapes=scratch,
            compiler_params=pltpu.CompilerParams(
                collective_id=0, has_side_effects=True, vmem_limit_bytes=56 * 1024 * 1024
            ),
        )(
            by_slab(observations), by_slab(obs_mask), obs_weight, classes, kappa_table,
            jnp.asarray(basis), jnp.asarray(modal),
        )
        return by_row(sol), by_row(res)

    in_specs = (P("days", "rows", None), P("days", "rows", None), P("rows", None), P("rows", None), P())
    out_specs = (P("days", "rows", None), P("days", "rows", None))
    return jax.shard_map(body, mesh=mesh, in_specs=in_specs, out_specs=out_specs, check_vma=False)
```

```python
import math

import jax
import jax.numpy as jnp
import numpy as np
from jax import lax
from jax.experimental import pallas as pl
from jax.experimental.pallas import tpu as pltpu
from jax.sharding import PartitionSpec as P

MESH = pl.DeviceIdType.MESH
DEG = 8
TIME_SHIFT = 0.05
HALF_OBS = 0.5
KAPPA_LOW = 0.02
KAPPA_HIGH = 2.0
WEIGHT_LOW = 0.5
WEIGHT_HIGH = 4.0
STENCIL_SCALE = 6.0
STENCIL_TOP = 16.0 / 3.0

Y = 4
TB = 32
RB = 4
COLS = 32
HALO = 8
K = (COLS + 2 * HALO) // 8
LANES = 128
GROUP = 4


def modal_constants(total):
    order = np.arange(1, total + 1, dtype=np.float64)
    phase = np.outer(order, order) % (2 * (total + 1))
    basis = np.sqrt(2.0 / (total + 1)) * np.sin(np.pi * phase / (total + 1))
    eig = 2.0 + TIME_SHIFT - 2.0 * np.cos(np.pi * order / (total + 1))
    lower = eig * KAPPA_LOW + HALF_OBS * WEIGHT_LOW
    upper = eig * (KAPPA_HIGH + STENCIL_TOP) + HALF_OBS * WEIGHT_HIGH
    centre, spread = 0.5 * (upper + lower), 0.5 * (upper - lower)
    rows = np.zeros((8, total), np.float32)
    for at, row in enumerate(
        (eig / STENCIL_SCALE, 1.0 / centre, centre / spread, 1.0 / spread, STENCIL_SCALE / eig)
    ):
        rows[at] = row
    return basis.astype(np.float32), rows


def make_kernel(Z, D):
    NT = TB * D
    ROWS = RB * Y
    J = Y * D
    WIDE = NT // LANES
    DBITS = D.bit_length() - 1
    SLABS = J // 4
    ER, EC = ROWS + 2 * HALO, COLS + 2 * HALO
    OWN = pl.ds(HALO, COLS)

    def kernel(
        obs_in, mask_in, weight_in, classes_in, kappa, basis_in, modal_in, sol, res,
        obs, mask, weight, classes, basis, modal,
        GE1, GE2, U, DX, G, KC, SC, NC, MK, NAT, NQ, NZ, NW, NV, PR, PS, XR, XS,
        TZ, TQ, TW, TV, FZ, FQ, FW, FV, PW, CW, CT, CN, SA, RS, sol_out, res_out,
        halo_send, halo_recv, near_send, near_recv, all_send, all_recv, cell_send, cell_recv,
        sum_send, sum_recv, load_sem, out_sem,
    ):
        ri, d = lax.axis_index("rows"), lax.axis_index("days")
        z, y = ri // Y, ri % Y
        j = y * D + (d ^ ((D - 1) * (y & 1)))
        top, bottom, left, right = z == 0, z == Z - 1, j == 0, j == J - 1

        def place(jt):
            yt = jt >> DBITS
            return yt, (jt & (D - 1)) ^ ((D - 1) * (yt & 1))

        def device(zt, jt):
            yt, dt = place(jt)
            return (zt * Y + yt, dt)

        north, south = lax.rem(z + Z - 1, Z), lax.rem(z + 1, Z)
        west, east = lax.rem(j + J - 1, J), lax.rem(j + 1, J)

        CN[...] = jnp.zeros_like(CN)
        loads = [
            pltpu.make_async_copy(src, dst, load_sem.at[i])
            for i, (src, dst) in enumerate((
                (weight_in, weight), (classes_in, classes), (obs_in, obs), (mask_in, mask),
                (basis_in, basis), (modal_in, modal),
            ))
        ]
        for load in loads:
            load.start()

        barrier = pltpu.get_barrier_semaphore()

        def greet(target):
            pl.semaphore_signal(barrier, inc=1, device_id=target, device_id_type=MESH)

        def greet_plane(i, c):
            greet(device(z, ((j + i) & (J - 1))))
            return c

        def greet_column(i, c):
            greet((((z + i) & (Z - 1)) * Y + y, d))
            return c

        lax.fori_loop(1, J, greet_plane, 0)
        lax.fori_loop(1, Z, greet_column, 0)
        for zt in (north, south):
            for jt in (west, east):
                greet(device(zt, jt))

        def full(v):
            return jnp.broadcast_to(v, (8, LANES))

        def swap(parts):
            lane = lax.broadcasted_iota(jnp.int32, parts[0].shape, 1)
            wide, even = lane < 64, (lane // 32) % 2 == 0
            t0 = jnp.where(wide, parts[0], pltpu.roll(parts[2], 64, 1))
            t2 = jnp.where(wide, pltpu.roll(parts[0], 64, 1), parts[2])
            t1 = jnp.where(wide, parts[1], pltpu.roll(parts[3], 64, 1))
            t3 = jnp.where(wide, pltpu.roll(parts[1], 64, 1), parts[3])
            d0 = jnp.where(even, t0, pltpu.roll(t1, 32, 1))
            d1 = jnp.where(even, pltpu.roll(t0, 96, 1), t1)
            d2 = jnp.where(even, t2, pltpu.roll(t3, 32, 1))
            d3 = jnp.where(even, pltpu.roll(t2, 96, 1), t3)
            return d0, d1, d2, d3

        loads[0].wait()
        loads[1].wait()
        slab = pl.ds(pl.multiple_of(d * LANES, LANES), LANES)
        cls = classes[:, slab]
        kap = jnp.zeros((RB, LANES), jnp.float32)
        for level in range(16):
            kap = jnp.where(cls == level, kappa[level], kap)
        own_w = weight[:, slab]
        sub8 = lax.broadcasted_iota(jnp.int32, (8, LANES), 0)
        cells = []
        for r in range(RB):
            w_row = jnp.broadcast_to(own_w[r : r + 1], (8, LANES))
            k_row = jnp.broadcast_to(kap[r : r + 1], (8, LANES))
            cells.append(jnp.where(sub8 == 0, w_row, k_row))
        for q, part in enumerate(swap(cells)):
            PW[q] = part

        def day_rows(i, r, t):
            return pl.ds(t * SLABS * RB + RB * i + r, 8, stride=SLABS * RB)

        def seen_rows(i, r):
            lanes = pl.ds(pl.multiple_of(i * LANES, LANES), LANES)
            seen = [mask[day_rows(i, r, t), :] for t in range(0, TB, 8)]
            return jnp.concatenate(seen, axis=0).astype(jnp.float32) * weight[r : r + 1, lanes]

        for load in loads[2:]:
            load.wait()

        def shuffle_rhs(i, c):
            rhs = []
            for r in range(RB):
                seen = [obs[day_rows(i, r, t), :] for t in range(0, TB, 8)]
                rhs.append(seen_rows(i, r) * jnp.concatenate(seen, axis=0))
            for q, part in enumerate(swap(rhs)):
                PR[4 * i + q] = part
            return c

        lax.fori_loop(0, SLABS, shuffle_rhs, 0)

        pl.semaphore_wait(barrier, (J - 1) + (Z - 1) + 4)

        def cell_copy(q):
            return pltpu.make_async_remote_copy(
                src_ref=PW.at[q], dst_ref=CW.at[y], send_sem=cell_send.at[q],
                recv_sem=cell_recv.at[y], device_id=device(z, 4 * d + q), device_id_type=MESH,
            )

        def cell_local(q):
            return pltpu.make_async_copy(PW.at[q], CW.at[y], cell_recv.at[y])

        for q in range(4):
            @pl.when(4 * d + q != j)
            def _():
                cell_copy(q).start()

            @pl.when(4 * d + q == j)
            def _():
                cell_local(q).start()

        def to_tile(src, dst, at, i):
            jt = ((j + i) & (J - 1))
            return pltpu.make_async_remote_copy(
                src_ref=src.at[jt], dst_ref=dst.at[y, pl.ds(pl.multiple_of(d * TB, TB), TB)],
                send_sem=all_send.at[at], recv_sem=all_recv.at[at],
                device_id=device(z, jt), device_id_type=MESH,
            )

        def to_days(src, dst, at, i):
            jt = ((j + i) & (J - 1))
            yt, dt = place(jt)
            return pltpu.make_async_remote_copy(
                src_ref=src.at[yt, pl.ds(pl.multiple_of(dt * TB, TB), TB)], dst_ref=dst.at[j],
                send_sem=all_send.at[at], recv_sem=all_recv.at[at],
                device_id=device(z, jt), device_id_type=MESH,
            )

        def send_range(copy, src, dst, at, low, high):
            def one(i, c):
                copy(src, dst, at, i).start()
                return c

            lax.fori_loop(low, high, one, 0)

        def own_tile(src, dst, at):
            pltpu.make_async_copy(
                src.at[j], dst.at[y, pl.ds(pl.multiple_of(d * TB, TB), TB)], all_recv.at[at]
            ).start()

        def own_days(src, dst, at):
            pltpu.make_async_copy(
                src.at[y, pl.ds(pl.multiple_of(d * TB, TB), TB)], dst.at[j], all_recv.at[at]
            ).start()

        def send_tile(src, dst, at):
            send_range(to_tile, src, dst, at, 1, J)
            own_tile(src, dst, at)

        def send_days(src, dst, at):
            send_range(to_days, src, dst, at, 1, J)
            own_days(src, dst, at)

        def all_wait(dst, at):
            pltpu.make_async_copy(dst, dst, all_recv.at[at]).wait()

        def all_wait_send(at):
            pltpu.make_async_copy(
                PR.at[pl.ds(0, J - 1)], PR.at[pl.ds(0, J - 1)], all_send.at[at]
            ).wait()

        SIDES, ENDS = (2, 3), (0, 1, 4, 5, 6, 7)
        ways = []
        for dz, dj in ((-1, 0), (1, 0), (0, -1), (0, 1), (-1, -1), (-1, 1), (1, -1), (1, 1)):
            to_ok, from_ok = True, True
            if dz:
                to_ok, from_ok = (~top, ~bottom) if dz < 0 else (~bottom, ~top)
            if dj:
                a, b = (~left, ~right) if dj < 0 else (~right, ~left)
                to_ok, from_ok = (a, b) if to_ok is True else (to_ok & a, from_ok & b)
            zt = z if dz == 0 else (north if dz < 0 else south)
            jt = j if dj == 0 else (west if dj < 0 else east)
            ways.append((dz, dj, device(zt, jt), to_ok, from_ok))

        def near_copy(at):
            return pltpu.make_async_remote_copy(
                src_ref=CT, dst_ref=CN.at[at], send_sem=near_send.at[at],
                recv_sem=near_recv.at[at], device_id=ways[at][2], device_id_type=MESH,
            )

        def halo_copy(ge, n, w, at):
            dz, dj, target, _, _ = ways[at]
            def span(delta, size):
                if delta == 0:
                    return pl.ds(HALO, size), pl.ds(HALO, size)
                if delta < 0:
                    return pl.ds(HALO, HALO), pl.ds(HALO + size, HALO)
                return pl.ds(size, HALO), pl.ds(0, HALO)

            (rs, rd), (cs, cd) = span(dz, ROWS), span(dj, COLS)
            return pltpu.make_async_remote_copy(
                src_ref=ge.at[w, rs, cs], dst_ref=ge.at[w, rd, cd],
                send_sem=halo_send.at[n, w, at], recv_sem=halo_recv.at[n, w, at],
                device_id=target, device_id_type=MESH,
            )

        def each_way(which, do, among=range(8)):
            for at in among:
                way = ways[at]

                @pl.when(way[which])
                def _():
                    do(at)

        def halo_start(ge, n, w):
            each_way(3, lambda at: halo_copy(ge, n, w, at).start())

        def halo_wait(ge, n, w, among):
            each_way(4, lambda at: halo_copy(ge, n, w, at).wait_recv(), among)

        def send_rhs(i, c):
            to_tile(PR, XR, 0, i).start()
            return c

        lax.fori_loop(1, J, send_rhs, 0)
        own_tile(PR, XR, 0)

        def shuffle_seen(i, c):
            for q, part in enumerate(swap([seen_rows(i, r) for r in range(RB)])):
                PS[4 * i + q] = part
            return c

        lax.fori_loop(0, SLABS, shuffle_seen, 0)

        for cond, rows, cols in (
            (top, pl.ds(0, HALO), pl.ds(0, EC)),
            (bottom, pl.ds(HALO + ROWS, HALO), pl.ds(0, EC)),
            (left, pl.ds(0, ER), pl.ds(0, HALO)),
            (right, pl.ds(0, ER), pl.ds(HALO + COLS, HALO)),
        ):
            @pl.when(cond)
            def _():
                for ge in (GE1, GE2):
                    for w in range(WIDE):
                        ge[w, rows, cols, :] = jnp.zeros((rows.size, cols.size, LANES), jnp.float32)


        for yt in range(Y):
            pltpu.make_async_copy(CW.at[yt], CW.at[yt], cell_recv.at[yt]).wait()
        packed = jnp.zeros((8, LANES), jnp.float32)
        for yt in range(Y):
            for f in range(2):
                packed = jnp.where(sub8 == Y * f + yt, CW[yt][f : f + 1], packed)
        CT[...] = packed
        each_way(3, lambda at: near_copy(at).start())

        column = lax.broadcasted_iota(jnp.int32, (8, LANES), 0) * K
        for k in range(K):
            outside = (left & (column + k < HALO)) | (right & (column + k >= HALO + COLS))
            MK[0, k] = jnp.zeros((8, LANES), jnp.float32)
            MK[1, k] = jnp.where(outside, 0.0, 1.0)

        def spread_tile(source, dz, dj):
            for f, scale, shift in ((0, HALF_OBS, 0.0), (1, STENCIL_SCALE, 36.0)):
                for yt in range(Y):
                    if (dz < 0 and RB * (yt + 1) <= ROWS - HALO) or (dz > 0 and RB * yt >= HALO):
                        continue
                    at = Y * f + yt
                    flat = jnp.broadcast_to(source[at : at + 1], (LANES, LANES)) * scale + shift
                    turned = jnp.transpose(flat).reshape(RB, COLS, LANES)
                    row = HALO + dz * ROWS + RB * yt
                    if dj == 0:
                        NC[f, row : row + RB, OWN, :] = turned
                    elif dj < 0:
                        NC[f, row : row + RB, 0:HALO, :] = turned[:, COLS - HALO :]
                    else:
                        NC[f, row : row + RB, HALO + COLS : EC, :] = turned[:, :HALO]

        spread_tile(packed, 0, 0)
        each_way(4, lambda at: near_copy(at).wait_recv())
        for at, way in enumerate(ways):
            spread_tile(CN[at], -way[0], -way[1])

        inv_eig = [full(modal[4:5, w * LANES : (w + 1) * LANES]) for w in range(WIDE)]

        def interleave_cells(e, c):
            for k in range(K):
                hc = NC[0, e, pl.ds(k, 8, stride=K), :]
                kc = NC[1, e, pl.ds(k, 8, stride=K), :]
                KC[e, k] = kc
                for w in range(WIDE):
                    SC[w, e, k] = hc * inv_eig[w] + kc
            return c

        lax.fori_loop(0, ER, interleave_cells, 0)

        def dot(a, b, dims):
            return lax.dot_general(
                a, b, (dims, ((), ())), precision=lax.Precision.HIGHEST,
                preferred_element_type=jnp.float32,
            )

        def to_modes(tile, put):
            def one(i, c):
                v = jnp.concatenate([tile(2 * i), tile(2 * i + 1)], axis=1)
                h = dot(jnp.transpose(v), basis[...], ((1,), (0,)))
                for w in range(WIDE):
                    put(w, 2 * RB * i, h[:, w * LANES : (w + 1) * LANES].reshape(2 * RB, COLS, LANES))
                return c

            lax.fori_loop(0, Y // 2, one, 0)

        def to_time(get, out):
            def one(i, c):
                v = [get(w, pl.ds(2 * RB * i, 2 * RB)).reshape(2 * RB * COLS, LANES) for w in range(WIDE)]
                t = dot(basis[...], jnp.concatenate(v, axis=1), ((1,), (1,)))
                out[2 * i] = t[:, :LANES]
                out[2 * i + 1] = t[:, LANES:]
                return c

            lax.fori_loop(0, Y // 2, one, 0)

        def coefficients(w):
            lanes = slice(w * LANES, (w + 1) * LANES)
            return [modal[i : i + 1, lanes] for i in range(4)]

        def rows_of(p, w, first, count):
            above = [U[p, w, first - 1, k] for k in range(K)]
            here = [U[p, w, first, k] for k in range(K)]
            for i in range(count):
                below = [U[p, w, first + 1 + i, k] for k in range(K)]
                b = [4.0 * here[k] + (above[k] + below[k]) for k in range(K)]
                line = [pltpu.roll(b[K - 1], 1, 0)] + b + [pltpu.roll(b[0], 7, 0)]
                yield i, here, [(line[k] + line[k + 2]) + 4.0 * b[k] for k in range(K)]
                above, here = here, below

        def begin(ge, w, low, count):
            ic, ie = full(coefficients(w)[1]), inv_eig[w]

            def one(i, c):
                for e in (low + 2 * i, low + 2 * i + 1):
                    for k in range(K):
                        g = ge[w, e, pl.ds(k, 8, stride=K), :]
                        G[w, e, k] = g * ie
                        u = g * ic
                        U[0, w, e, k] = u
                        DX[w, e, k] = u
                return c

            lax.fori_loop(0, count // 2, one, 0)

        def sweeps(w, rows):
            eig6, _, stretch, inv_spread = coefficients(w)

            def sweep(n, ratio):
                p = n % 2
                ratio_next = 1.0 / (2.0 * stretch - ratio)
                momentum = full(ratio_next * ratio)
                step = full(2.0 * ratio_next * inv_spread * eig6)

                def advance(first, count, edge):
                    for at, v, h in rows_of(p, w, first, count):
                        e = first + at
                        inside = 1
                        if edge:
                            above, below = top & (e < HALO), bottom & (e >= HALO + ROWS)
                            inside = jnp.where(above | below, 0, 1)
                        for k in range(K):
                            dx = step * ((G[w, e, k] - SC[w, e, k] * v[k]) + h[k])
                            dx = (momentum * DX[w, e, k] + dx) * MK[inside, k]
                            DX[w, e, k] = dx
                            U[1 - p, w, e, k] = v[k] + dx

                rows(n, advance)
                return ratio_next

            lax.fori_loop(0, DEG - 1, sweep, 1.0 / stretch)

        def inner(ge, n_halo, w):
            halo_wait(ge, n_halo, w, SIDES)
            begin(ge, w, HALO, ROWS)

            def rows(n, advance):
                def one(i, c):
                    advance(HALO + 1 + n + 2 * i, 2, False)
                    return c

                lax.fori_loop(0, ROWS // 2 - 1 - n, one, 0)

            sweeps(w, rows)

        def outer(ge, n_halo, w):
            halo_wait(ge, n_halo, w, ENDS)
            begin(ge, w, 0, HALO)
            begin(ge, w, HALO + ROWS, HALO)

            def rows(n, advance):
                def one(i, c):
                    upper = n + 1 + GROUP * i
                    lower = ROWS + HALO - 1 - n + GROUP * i - HALO
                    advance(jnp.where(i < HALO // GROUP, upper, lower), GROUP, True)
                    return c

                lax.fori_loop(0, 2 * HALO // GROUP, one, 0)

            sweeps(w, rows)

        def keep_rows(w, keep):
            def one(i, c):
                for r in (2 * i, 2 * i + 1):
                    for k in range(K):
                        keep[w, r, pl.ds(k, 8, stride=K), :] = U[(DEG - 1) % 2, w, r + HALO, k]
                return c

            lax.fori_loop(0, ROWS // 2, one, 0)

        def stencil_part(w):
            eig6 = full(coefficients(w)[0])

            def one(i, c):
                first = GROUP * i
                for at, v, h in rows_of((DEG - 1) % 2, w, first + HALO, GROUP):
                    r = first + at
                    for k in range(K):
                        NQ[w, r, pl.ds(k, 8, stride=K), :] = eig6 * (KC[r + HALO, k] * v[k] - h[k])
                return c

            lax.fori_loop(0, ROWS // GROUP, one, 0)

        def pack(parts):
            out = jnp.zeros((8, LANES), jnp.float32)
            for at, part in enumerate(parts):
                out = jnp.where(sub8 == at, jnp.sum(part, axis=0, keepdims=True), out)
            return out

        stages = (
            (Z, z, lambda i: (((z + i) & (Z - 1)) * Y + y, d)),
            (D, d, lambda i: (ri, (d + i) & (D - 1))),
            (Y, y, lambda i: (z * Y + ((y + i) & (Y - 1)), d)),
        )

        def sum_start(at, stage, value):
            count, me, target = stages[stage]
            SA[at, stage] = value
            RS[at, stage, me] = value

            def one(i, c):
                pltpu.make_async_remote_copy(
                    src_ref=SA.at[at, stage], dst_ref=RS.at[at, stage, me],
                    send_sem=sum_send.at[at, stage], recv_sem=sum_recv.at[at, stage],
                    device_id=target(i), device_id_type=MESH,
                ).start()
                return c

            lax.fori_loop(1, count, one, 0)

        def sum_end(at, stage):
            count = stages[stage][0]
            part = RS.at[at, stage, pl.ds(0, count - 1)]
            for side in (sum_recv, sum_send):
                pltpu.make_async_copy(part, part, side.at[at, stage]).wait()
            total = RS[at, stage, 0]
            for i in range(1, count):
                total = total + RS[at, stage, i]
            return total

        def sum_values(total):
            return [jnp.sum(total[i : i + 1], axis=1, keepdims=True) for i in range(3)]

        zero = jnp.zeros((8, LANES), jnp.float32)

        def fold_cells(v):
            return jnp.sum(v.reshape(COLS // 8, 8, LANES), axis=0)

        def put_first(w, row, v):
            GE1[w, pl.ds(HALO + row, 2 * RB), OWN, :] = v

        def put_seen(w, row, v):
            NAT[w, pl.ds(row, 2 * RB)] = v

        all_wait(XR, 0)
        to_modes(lambda i: XR[i], put_first)
        for w in range(WIDE):
            halo_start(GE1, 0, w)
        send_tile(PS, XS, 1)
        for w in range(WIDE):
            inner(GE1, 0, w)
        for w in range(WIDE):
            outer(GE1, 0, w)
            keep_rows(w, NZ)
            stencil_part(w)
        to_time(lambda w, rows: NZ[w, rows, OWN, :], TZ)
        all_wait(XS, 1)
        to_modes(lambda i: TZ[i] * XS[i], put_seen)

        sums = (zero, zero)
        for w in range(WIDE):
            def first_image(r, acc):
                fit, curve = acc
                zh = NZ[w, r, OWN, :]
                q = NQ[w, r, OWN, :] + NAT[w, r]
                GE2[w, r + HALO, OWN, :] = q
                return fit + fold_cells(GE1[w, r + HALO, OWN, :] * zh), curve + fold_cells(zh * q)

            sums = lax.fori_loop(0, ROWS, first_image, sums)
            halo_start(GE2, 1, w)
        sum_start(0, 0, pack(sums))
        send_days(TZ, FZ, 2)
        to_time(lambda w, rows: GE2[w, pl.ds(rows.start + HALO, rows.size), OWN, :], TQ)
        send_days(TQ, FQ, 3)

        sum_start(0, 1, sum_end(0, 0))
        for w in range(WIDE):
            inner(GE2, 1, w)
        sum_start(0, 2, sum_end(0, 1))
        for w in range(WIDE):
            outer(GE2, 1, w)
            keep_rows(w, NW)
            if w + 1 < WIDE:
                stencil_part(w)
        to_time(lambda w, rows: NW[w, rows, OWN, :], TW)
        send_days(TW, FW, 4)
        stencil_part(WIDE - 1)
        to_modes(lambda i: TW[i] * XS[i], put_seen)
        fit0, curve0, _ = sum_values(sum_end(0, 2))
        alpha0 = fit0 / curve0

        sums = (zero, zero, zero)
        for w in range(WIDE):
            def second_image(r, acc):
                fit, curve, cross = acc
                wh, g = NW[w, r, OWN, :], GE2[w, r + HALO, OWN, :]
                q = NQ[w, r, OWN, :] + NAT[w, r]
                NV[w, r] = q
                z1 = NZ[w, r, OWN, :] - alpha0 * wh
                r1 = GE1[w, r + HALO, OWN, :] - alpha0 * g
                return (
                    fit + fold_cells(r1 * z1), curve + fold_cells(z1 * (g - alpha0 * q)),
                    cross + fold_cells(z1 * g),
                )

            sums = lax.fori_loop(0, ROWS, second_image, sums)
        sum_start(1, 0, pack(sums))
        to_time(lambda w, rows: NV[w, rows], TV)
        own_days(TV, FV, 5)
        send_range(to_days, TV, FV, 5, 1, 8)
        sum_start(1, 1, sum_end(1, 0))
        send_range(to_days, TV, FV, 5, 8, 20)
        sum_start(1, 2, sum_end(1, 1))
        send_range(to_days, TV, FV, 5, 20, J)
        fit1, curve1, cross1 = sum_values(sum_end(1, 2))
        beta = fit1 / fit0
        alpha1 = fit1 / (curve1 + 2.0 * beta * cross1 + beta * beta * curve0)
        c_old = alpha0 + alpha1 + alpha1 * beta
        c_new = alpha0 * alpha1

        def finish(part):
            def one(i, c):
                values = []
                for q in range(4):
                    at = 4 * i + q
                    if part == 0:
                        values.append(c_old * FZ[at] - c_new * FW[at])
                    else:
                        values.append(PR[at] - c_old * FQ[at] + c_new * FV[at])
                for r, v in enumerate(swap(values)):
                    for t in range(0, TB, 8):
                        (sol_out, res_out)[part][day_rows(i, r, t), :] = v[t : t + 8]
                return c

            lax.fori_loop(0, SLABS, one, 0)

        all_wait(FZ, 2)
        all_wait(FW, 4)
        finish(0)
        outs = [
            pltpu.make_async_copy(src, dst, out_sem.at[i])
            for i, (src, dst) in enumerate(((sol_out, sol), (res_out, res)))
        ]
        outs[0].start()
        all_wait(FQ, 3)
        all_wait(FV, 5)
        finish(1)
        outs[1].start()

        for at in range(6):
            all_wait_send(at)
        for q in range(4):
            @pl.when(4 * d + q != j)
            def _():
                cell_copy(q).wait_send()
        each_way(3, lambda at: near_copy(at).wait_send())
        for n, ge in enumerate((GE1, GE2)):
            for w in range(WIDE):
                each_way(3, lambda at: halo_copy(ge, n, w, at).wait_send())
        for out in outs:
            out.wait()

    f32 = jnp.float32
    extended = pltpu.VMEM((WIDE, ER, EC, LANES), f32)
    strip = pltpu.VMEM((WIDE, ROWS, EC, LANES), f32)
    flat = pltpu.VMEM((WIDE, ROWS, COLS, LANES), f32)
    fields = pltpu.VMEM((WIDE, ER, K, 8, LANES), f32)
    cell = pltpu.VMEM((ER, K, 8, LANES), f32)
    days = pltpu.VMEM((J, TB, LANES), f32)
    tile = pltpu.VMEM((Y, NT, LANES), f32)
    dma = pltpu.SemaphoreType.DMA
    given = pltpu.VMEM((TB * SLABS * RB, LANES), f32)
    scratch = [
        given, pltpu.VMEM((TB * SLABS * RB, LANES), jnp.int32), pltpu.VMEM((RB, J * COLS), f32),
        pltpu.VMEM((RB, J * COLS), jnp.int32), pltpu.VMEM((NT, NT), f32), pltpu.VMEM((8, NT), f32),
        extended, extended, pltpu.VMEM((2, WIDE, ER, K, 8, LANES), f32),
        fields, fields, cell, fields, pltpu.VMEM((2, ER, EC, LANES), f32),
        pltpu.VMEM((2, K, 8, LANES), f32), flat, strip, strip, strip, flat, days, days, tile, tile,
        tile, tile, tile, tile, days, days, days, days,
        pltpu.VMEM((4, 8, LANES), f32), pltpu.VMEM((Y, 8, LANES), f32),
        pltpu.VMEM((8, LANES), f32), pltpu.VMEM((8, 8, LANES), f32),
        pltpu.VMEM((2, 3, 8, LANES), f32), pltpu.VMEM((2, 3, max(Z, D, Y), 8, LANES), f32), given, given,
        dma((2, WIDE, 8)), dma((2, WIDE, 8)), dma((8,)), dma((8,)), dma((6,)), dma((6,)),
        dma((4,)), dma((Y,)), dma((2, 3)), dma((2, 3)), dma((6,)), dma((2,)),
    ]
    return kernel, scratch


def solution(mesh):
    Z = mesh.shape["rows"] // Y
    D = mesh.shape["days"]
    kernel, scratch = make_kernel(Z, D)
    basis, modal = modal_constants(TB * D)
    slabs = Y * D // 4
    smem = pl.BlockSpec(memory_space=pltpu.SMEM)
    hbm = pl.BlockSpec(memory_space=pl.ANY)

    def by_slab(array):
        array = array.reshape(TB, RB, slabs, LANES)
        return jnp.transpose(array, (0, 2, 1, 3)).reshape(TB * slabs * RB, LANES)

    def by_row(array):
        array = array.reshape(TB, slabs, RB, LANES)
        return jnp.transpose(array, (0, 2, 1, 3)).reshape(TB, RB, slabs * LANES)

    def body(observations, obs_mask, obs_weight, classes, kappa_table):
        shape = jax.ShapeDtypeStruct((TB * slabs * RB, LANES), jnp.float32)
        sol, res = pl.pallas_call(
            kernel,
            out_shape=(shape, shape),
            in_specs=[hbm] * 4 + [smem] + [hbm] * 2,
            out_specs=(hbm, hbm),
            scratch_shapes=scratch,
            compiler_params=pltpu.CompilerParams(
                collective_id=0, has_side_effects=True, vmem_limit_bytes=56 * 1024 * 1024
            ),
        )(
            by_slab(observations), by_slab(obs_mask), obs_weight, classes, kappa_table,
            jnp.asarray(basis), jnp.asarray(modal),
        )
        return by_row(sol), by_row(res)

    in_specs = (P("days", "rows", None), P("days", "rows", None), P("rows", None), P("rows", None), P())
    out_specs = (P("days", "rows", None), P("days", "rows", None))
    return jax.shard_map(body, mesh=mesh, in_specs=in_specs, out_specs=out_specs, check_vma=False)
```

```python
import math

import jax
import jax.numpy as jnp
import numpy as np
from jax import lax
from jax.experimental import pallas as pl
from jax.experimental.pallas import tpu as pltpu
from jax.sharding import PartitionSpec as P

MESH = pl.DeviceIdType.MESH
DEG = 8
TIME_SHIFT = 0.05
HALF_OBS = 0.5
KAPPA_LOW = 0.02
KAPPA_HIGH = 2.0
WEIGHT_LOW = 0.5
WEIGHT_HIGH = 4.0
STENCIL_SCALE = 6.0
STENCIL_TOP = 16.0 / 3.0

Y = 4
TB = 32
RB = 4
COLS = 32
HALO = 8
K = (COLS + 2 * HALO) // 8
LANES = 128
GROUP = 4


def modal_constants(total):
    order = np.arange(1, total + 1, dtype=np.float64)
    phase = np.outer(order, order) % (2 * (total + 1))
    basis = np.sqrt(2.0 / (total + 1)) * np.sin(np.pi * phase / (total + 1))
    eig = 2.0 + TIME_SHIFT - 2.0 * np.cos(np.pi * order / (total + 1))
    lower = eig * KAPPA_LOW + HALF_OBS * WEIGHT_LOW
    upper = eig * (KAPPA_HIGH + STENCIL_TOP) + HALF_OBS * WEIGHT_HIGH
    centre, spread = 0.5 * (upper + lower), 0.5 * (upper - lower)
    rows = np.zeros((8, total), np.float32)
    for at, row in enumerate(
        (eig / STENCIL_SCALE, 1.0 / centre, centre / spread, 1.0 / spread, STENCIL_SCALE / eig)
    ):
        rows[at] = row
    return basis.astype(np.float32), rows


def make_kernel(Z, D):
    NT = TB * D
    ROWS = RB * Y
    J = Y * D
    WIDE = NT // LANES
    DBITS = D.bit_length() - 1
    CBITS = (NT // COLS).bit_length() - 1
    SLABS = J // 4
    ER, EC = ROWS + 2 * HALO, COLS + 2 * HALO
    OWN = pl.ds(HALO, COLS)

    def kernel(
        obs_in, mask_in, weight_in, classes_in, kappa, basis_in, modal_in, sol, res,
        obs, mask, weight, classes, basis, modal,
        GE1, GE2, U, DX, G, KC, SC, NC, MK, NAT, NQ, NZ, NW, PR, PS, XR, XS,
        TZ, TQ, TW, TV, FZ, FQ, FW, FV, PW, CW, CT, CN, SA, RS, sol_out, res_out, RL, AZ, AQ, AW,
        halo_send, halo_recv, near_send, near_recv, all_send, all_recv, cell_send, cell_recv,
        sum_send, sum_recv, load_sem, out_sem,
    ):
        ri, d = lax.axis_index("rows"), lax.axis_index("days")
        z, y = ri // Y, ri % Y
        j = y * D + (d ^ ((D - 1) * (y & 1)))
        top, bottom, left, right = z == 0, z == Z - 1, j == 0, j == J - 1

        def place(jt):
            yt = jt >> DBITS
            return yt, (jt & (D - 1)) ^ ((D - 1) * (yt & 1))

        def device(zt, jt):
            yt, dt = place(jt)
            return (zt * Y + yt, dt)

        north, south = lax.rem(z + Z - 1, Z), lax.rem(z + 1, Z)
        west, east = lax.rem(j + J - 1, J), lax.rem(j + 1, J)

        CN[...] = jnp.zeros_like(CN)
        loads = [
            pltpu.make_async_copy(src, dst, load_sem.at[i])
            for i, (src, dst) in enumerate((
                (weight_in, weight), (classes_in, classes), (obs_in, obs), (mask_in, mask),
                (basis_in, basis), (modal_in, modal),
            ))
        ]
        for load in loads:
            load.start()

        barrier = pltpu.get_barrier_semaphore()

        def greet(target):
            pl.semaphore_signal(barrier, inc=1, device_id=target, device_id_type=MESH)

        def greet_plane(i, c):
            greet(device(z, ((j + i) & (J - 1))))
            return c

        def greet_column(i, c):
            greet((((z + i) & (Z - 1)) * Y + y, d))
            return c

        lax.fori_loop(1, J, greet_plane, 0)
        lax.fori_loop(1, Z, greet_column, 0)
        for zt in (north, south):
            for jt in (west, east):
                greet(device(zt, jt))

        def full(v):
            return jnp.broadcast_to(v, (8, LANES))

        def swap(parts):
            lane = lax.broadcasted_iota(jnp.int32, parts[0].shape, 1)
            wide, even = lane < 64, (lane // 32) % 2 == 0
            t0 = jnp.where(wide, parts[0], pltpu.roll(parts[2], 64, 1))
            t2 = jnp.where(wide, pltpu.roll(parts[0], 64, 1), parts[2])
            t1 = jnp.where(wide, parts[1], pltpu.roll(parts[3], 64, 1))
            t3 = jnp.where(wide, pltpu.roll(parts[1], 64, 1), parts[3])
            d0 = jnp.where(even, t0, pltpu.roll(t1, 32, 1))
            d1 = jnp.where(even, pltpu.roll(t0, 96, 1), t1)
            d2 = jnp.where(even, t2, pltpu.roll(t3, 32, 1))
            d3 = jnp.where(even, pltpu.roll(t2, 96, 1), t3)
            return d0, d1, d2, d3

        loads[0].wait()
        loads[1].wait()
        slab = pl.ds(pl.multiple_of(d * LANES, LANES), LANES)
        cls = classes[:, slab]
        kap = jnp.zeros((RB, LANES), jnp.float32)
        for level in range(16):
            kap = jnp.where(cls == level, kappa[level], kap)
        own_w = weight[:, slab]
        sub8 = lax.broadcasted_iota(jnp.int32, (8, LANES), 0)
        cells = []
        for r in range(RB):
            w_row = jnp.broadcast_to(own_w[r : r + 1], (8, LANES))
            k_row = jnp.broadcast_to(kap[r : r + 1], (8, LANES))
            cells.append(jnp.where(sub8 == 0, w_row, k_row))
        for q, part in enumerate(swap(cells)):
            PW[q] = part

        def day_rows(i, r, t):
            return pl.ds(t * SLABS * RB + RB * i + r, 8, stride=SLABS * RB)

        def seen_rows(i, r):
            lanes = pl.ds(pl.multiple_of(i * LANES, LANES), LANES)
            seen = [mask[day_rows(i, r, t), :] for t in range(0, TB, 8)]
            return jnp.concatenate(seen, axis=0).astype(jnp.float32) * weight[r : r + 1, lanes]

        for load in loads[2:]:
            load.wait()

        def shuffle_rhs(i, c):
            rhs = []
            for r in range(RB):
                seen = [obs[day_rows(i, r, t), :] for t in range(0, TB, 8)]
                rhs.append(seen_rows(i, r) * jnp.concatenate(seen, axis=0))
                RL[i, r] = rhs[r]
            for q, part in enumerate(swap(rhs)):
                PR[4 * i + q] = part
            return c

        lax.fori_loop(0, SLABS, shuffle_rhs, 0)

        pl.semaphore_wait(barrier, (J - 1) + (Z - 1) + 4)

        def cell_copy(q):
            return pltpu.make_async_remote_copy(
                src_ref=PW.at[q], dst_ref=CW.at[y], send_sem=cell_send.at[q],
                recv_sem=cell_recv.at[y], device_id=device(z, 4 * d + q), device_id_type=MESH,
            )

        def cell_local(q):
            return pltpu.make_async_copy(PW.at[q], CW.at[y], cell_recv.at[y])

        for q in range(4):
            @pl.when(4 * d + q != j)
            def _():
                cell_copy(q).start()

            @pl.when(4 * d + q == j)
            def _():
                cell_local(q).start()

        def to_tile(src, dst, at, i):
            jt = ((j + i) & (J - 1))
            return pltpu.make_async_remote_copy(
                src_ref=src.at[jt], dst_ref=dst.at[y, pl.ds(pl.multiple_of(d * TB, TB), TB)],
                send_sem=all_send.at[at], recv_sem=all_recv.at[at],
                device_id=device(z, jt), device_id_type=MESH,
            )

        def to_days(src, dst, at, i):
            jt = ((j + i) & (J - 1))
            yt, dt = place(jt)
            return pltpu.make_async_remote_copy(
                src_ref=src.at[yt, pl.ds(pl.multiple_of(dt * TB, TB), TB)], dst_ref=dst.at[j],
                send_sem=all_send.at[at], recv_sem=all_recv.at[at],
                device_id=device(z, jt), device_id_type=MESH,
            )

        def send_range(copy, src, dst, at, low, high):
            def one(i, c):
                copy(src, dst, at, i).start()
                return c

            lax.fori_loop(low, high, one, 0)

        def own_tile(src, dst, at):
            pltpu.make_async_copy(
                src.at[j], dst.at[y, pl.ds(pl.multiple_of(d * TB, TB), TB)], all_recv.at[at]
            ).start()

        def own_days(src, dst, at):
            pltpu.make_async_copy(
                src.at[y, pl.ds(pl.multiple_of(d * TB, TB), TB)], dst.at[j], all_recv.at[at]
            ).start()

        def send_tile(src, dst, at):
            send_range(to_tile, src, dst, at, 1, J)
            own_tile(src, dst, at)

        def send_days(src, dst, at):
            send_range(to_days, src, dst, at, 1, J)
            own_days(src, dst, at)

        def all_wait(dst, at):
            pltpu.make_async_copy(dst, dst, all_recv.at[at]).wait()

        def all_wait_send(at):
            pltpu.make_async_copy(
                PR.at[pl.ds(0, J - 1)], PR.at[pl.ds(0, J - 1)], all_send.at[at]
            ).wait()

        SIDES, ENDS = (2, 3), (0, 1, 4, 5, 6, 7)
        ways = []
        for dz, dj in ((-1, 0), (1, 0), (0, -1), (0, 1), (-1, -1), (-1, 1), (1, -1), (1, 1)):
            to_ok, from_ok = True, True
            if dz:
                to_ok, from_ok = (~top, ~bottom) if dz < 0 else (~bottom, ~top)
            if dj:
                a, b = (~left, ~right) if dj < 0 else (~right, ~left)
                to_ok, from_ok = (a, b) if to_ok is True else (to_ok & a, from_ok & b)
            zt = z if dz == 0 else (north if dz < 0 else south)
            jt = j if dj == 0 else (west if dj < 0 else east)
            ways.append((dz, dj, device(zt, jt), to_ok, from_ok))

        def near_copy(at):
            return pltpu.make_async_remote_copy(
                src_ref=CT, dst_ref=CN.at[at], send_sem=near_send.at[at],
                recv_sem=near_recv.at[at], device_id=ways[at][2], device_id_type=MESH,
            )

        def halo_copy(ge, n, w, at):
            dz, dj, target, _, _ = ways[at]
            def span(delta, size):
                if delta == 0:
                    return pl.ds(HALO, size), pl.ds(HALO, size)
                if delta < 0:
                    return pl.ds(HALO, HALO), pl.ds(HALO + size, HALO)
                return pl.ds(size, HALO), pl.ds(0, HALO)

            (rs, rd), (cs, cd) = span(dz, ROWS), span(dj, COLS)
            return pltpu.make_async_remote_copy(
                src_ref=ge.at[w, rs, cs], dst_ref=ge.at[w, rd, cd],
                send_sem=halo_send.at[n, w, at], recv_sem=halo_recv.at[n, w, at],
                device_id=target, device_id_type=MESH,
            )

        def each_way(which, do, among=range(8)):
            for at in among:
                way = ways[at]

                @pl.when(way[which])
                def _():
                    do(at)

        def halo_start(ge, n, w):
            each_way(3, lambda at: halo_copy(ge, n, w, at).start())

        def halo_wait(ge, n, w, among):
            each_way(4, lambda at: halo_copy(ge, n, w, at).wait_recv(), among)

        def send_rhs(i, c):
            to_tile(PR, XR, 0, i).start()
            return c

        lax.fori_loop(1, J, send_rhs, 0)
        own_tile(PR, XR, 0)

        def shuffle_seen(i, c):
            for q, part in enumerate(swap([seen_rows(i, r) for r in range(RB)])):
                PS[4 * i + q] = part
            return c

        lax.fori_loop(0, SLABS, shuffle_seen, 0)

        for cond, rows, cols in (
            (top, pl.ds(0, HALO), pl.ds(0, EC)),
            (bottom, pl.ds(HALO + ROWS, HALO), pl.ds(0, EC)),
            (left, pl.ds(0, ER), pl.ds(0, HALO)),
            (right, pl.ds(0, ER), pl.ds(HALO + COLS, HALO)),
        ):
            @pl.when(cond)
            def _():
                for ge in (GE1, GE2):
                    for w in range(WIDE):
                        ge[w, rows, cols, :] = jnp.zeros((rows.size, cols.size, LANES), jnp.float32)


        for yt in range(Y):
            pltpu.make_async_copy(CW.at[yt], CW.at[yt], cell_recv.at[yt]).wait()
        packed = jnp.zeros((8, LANES), jnp.float32)
        for yt in range(Y):
            for f in range(2):
                packed = jnp.where(sub8 == Y * f + yt, CW[yt][f : f + 1], packed)
        CT[...] = packed
        each_way(3, lambda at: near_copy(at).start())

        column = lax.broadcasted_iota(jnp.int32, (8, LANES), 0) * K
        for k in range(K):
            outside = (left & (column + k < HALO)) | (right & (column + k >= HALO + COLS))
            MK[0, k] = jnp.zeros((8, LANES), jnp.float32)
            MK[1, k] = jnp.where(outside, 0.0, 1.0)

        def spread_tile(source, dz, dj):
            for f, scale, shift in ((0, HALF_OBS, 0.0), (1, STENCIL_SCALE, 36.0)):
                for yt in range(Y):
                    if (dz < 0 and RB * (yt + 1) <= ROWS - HALO) or (dz > 0 and RB * yt >= HALO):
                        continue
                    at = Y * f + yt
                    flat = jnp.broadcast_to(source[at : at + 1], (LANES, LANES)) * scale + shift
                    turned = jnp.transpose(flat).reshape(RB, COLS, LANES)
                    row = HALO + dz * ROWS + RB * yt
                    if dj == 0:
                        NC[f, row : row + RB, OWN, :] = turned
                    elif dj < 0:
                        NC[f, row : row + RB, 0:HALO, :] = turned[:, COLS - HALO :]
                    else:
                        NC[f, row : row + RB, HALO + COLS : EC, :] = turned[:, :HALO]

        spread_tile(packed, 0, 0)
        each_way(4, lambda at: near_copy(at).wait_recv())
        for at, way in enumerate(ways):
            spread_tile(CN[at], -way[0], -way[1])

        inv_eig = [full(modal[4:5, w * LANES : (w + 1) * LANES]) for w in range(WIDE)]

        def interleave_cells(e, c):
            for k in range(K):
                hc = NC[0, e, pl.ds(k, 8, stride=K), :]
                kc = NC[1, e, pl.ds(k, 8, stride=K), :]
                KC[e, k] = kc
                for w in range(WIDE):
                    SC[w, e, k] = hc * inv_eig[w] + kc
            return c

        lax.fori_loop(0, ER, interleave_cells, 0)

        def dot(a, b, dims):
            return lax.dot_general(
                a, b, (dims, ((), ())), precision=lax.Precision.HIGHEST,
                preferred_element_type=jnp.float32,
            )

        def to_modes(tile, put):
            def one(i, c):
                v = jnp.concatenate([tile(2 * i), tile(2 * i + 1)], axis=1)
                h = dot(jnp.transpose(v), basis[...], ((1,), (0,)))
                for w in range(WIDE):
                    put(w, 2 * RB * i, h[:, w * LANES : (w + 1) * LANES].reshape(2 * RB, COLS, LANES))
                return c

            lax.fori_loop(0, Y // 2, one, 0)

        def to_time(get, out, extra=None):
            def one(i, c):
                v = [get(w, pl.ds(2 * RB * i, 2 * RB)).reshape(2 * RB * COLS, LANES) for w in range(WIDE)]
                t = dot(basis[...], jnp.concatenate(v, axis=1), ((1,), (1,)))
                for half in range(2):
                    part = t[:, half * LANES : (half + 1) * LANES]
                    out[2 * i + half] = part if extra is None else part + extra(2 * i + half)
                return c

            lax.fori_loop(0, Y // 2, one, 0)

        def coefficients(w):
            lanes = slice(w * LANES, (w + 1) * LANES)
            return [modal[i : i + 1, lanes] for i in range(4)]

        def rows_of(p, w, first, count):
            above = [U[p, w, first - 1, k] for k in range(K)]
            here = [U[p, w, first, k] for k in range(K)]
            for i in range(count):
                below = [U[p, w, first + 1 + i, k] for k in range(K)]
                b = [4.0 * here[k] + (above[k] + below[k]) for k in range(K)]
                line = [pltpu.roll(b[K - 1], 1, 0)] + b + [pltpu.roll(b[0], 7, 0)]
                yield i, here, [(line[k] + line[k + 2]) + 4.0 * b[k] for k in range(K)]
                above, here = here, below

        def begin(ge, w, low, count):
            ic, ie = full(coefficients(w)[1]), inv_eig[w]

            def one(i, c):
                for e in (low + 2 * i, low + 2 * i + 1):
                    for k in range(K):
                        g = ge[w, e, pl.ds(k, 8, stride=K), :]
                        G[w, e, k] = g * ie
                        u = g * ic
                        U[0, w, e, k] = u
                        DX[w, e, k] = u
                return c

            lax.fori_loop(0, count // 2, one, 0)

        def sweeps(w, rows):
            eig6, _, stretch, inv_spread = coefficients(w)

            def sweep(n, ratio):
                p = n % 2
                ratio_next = 1.0 / (2.0 * stretch - ratio)
                momentum = full(ratio_next * ratio)
                step = full(2.0 * ratio_next * inv_spread * eig6)

                def advance(first, count, edge):
                    for at, v, h in rows_of(p, w, first, count):
                        e = first + at
                        inside = 1
                        if edge:
                            above, below = top & (e < HALO), bottom & (e >= HALO + ROWS)
                            inside = jnp.where(above | below, 0, 1)
                        for k in range(K):
                            dx = step * ((G[w, e, k] - SC[w, e, k] * v[k]) + h[k])
                            dx = (momentum * DX[w, e, k] + dx) * MK[inside, k]
                            DX[w, e, k] = dx
                            U[1 - p, w, e, k] = v[k] + dx

                rows(n, advance)
                return ratio_next

            lax.fori_loop(0, DEG - 1, sweep, 1.0 / stretch)

        def inner(ge, n_halo, w):
            halo_wait(ge, n_halo, w, SIDES)
            begin(ge, w, HALO, ROWS)

            def rows(n, advance):
                def one(i, c):
                    advance(HALO + 1 + n + 2 * i, 2, False)
                    return c

                lax.fori_loop(0, ROWS // 2 - 1 - n, one, 0)

            sweeps(w, rows)

        def outer(ge, n_halo, w):
            halo_wait(ge, n_halo, w, ENDS)
            begin(ge, w, 0, HALO)
            begin(ge, w, HALO + ROWS, HALO)

            def rows(n, advance):
                def one(i, c):
                    upper = n + 1 + GROUP * i
                    lower = ROWS + HALO - 1 - n + GROUP * i - HALO
                    advance(jnp.where(i < HALO // GROUP, upper, lower), GROUP, True)
                    return c

                lax.fori_loop(0, 2 * HALO // GROUP, one, 0)

            sweeps(w, rows)

        def keep_rows(w, keep):
            def one(i, c):
                for r in (2 * i, 2 * i + 1):
                    for k in range(K):
                        keep[w, r, pl.ds(k, 8, stride=K), :] = U[(DEG - 1) % 2, w, r + HALO, k]
                return c

            lax.fori_loop(0, ROWS // 2, one, 0)

        def stencil_part(w):
            eig6 = full(coefficients(w)[0])

            def one(i, c):
                first = GROUP * i
                for at, v, h in rows_of((DEG - 1) % 2, w, first + HALO, GROUP):
                    r = first + at
                    for k in range(K):
                        NQ[w, r, pl.ds(k, 8, stride=K), :] = eig6 * (KC[r + HALO, k] * v[k] - h[k])
                return c

            lax.fori_loop(0, ROWS // GROUP, one, 0)

        def pack(parts):
            out = jnp.zeros((8, LANES), jnp.float32)
            for at, part in enumerate(parts):
                out = jnp.where(sub8 == at, jnp.sum(part, axis=0, keepdims=True), out)
            return out

        stages = (
            (D, d, lambda i: (ri, (d + i) & (D - 1))),
            (Y, y, lambda i: (z * Y + ((y + i) & (Y - 1)), d)),
            (Z, z, lambda i: (((z + i) & (Z - 1)) * Y + y, d)),
        )

        def sum_start(at, stage, value):
            count, me, target = stages[stage]
            SA[at, stage] = value
            RS[at, stage, me] = value

            def one(i, c):
                pltpu.make_async_remote_copy(
                    src_ref=SA.at[at, stage], dst_ref=RS.at[at, stage, me],
                    send_sem=sum_send.at[at, stage], recv_sem=sum_recv.at[at, stage],
                    device_id=target(i), device_id_type=MESH,
                ).start()
                return c

            lax.fori_loop(1, count, one, 0)

        def sum_end(at, stage):
            count = stages[stage][0]
            part = RS.at[at, stage, pl.ds(0, count - 1)]
            for side in (sum_recv, sum_send):
                pltpu.make_async_copy(part, part, side.at[at, stage]).wait()
            total = RS[at, stage, 0]
            for i in range(1, count):
                total = total + RS[at, stage, i]
            return total

        def sum_values(total):
            return [jnp.sum(total[i : i + 1], axis=1, keepdims=True) for i in range(3)]

        zero = jnp.zeros((8, LANES), jnp.float32)

        def fold_cells(v):
            return jnp.sum(v.reshape(COLS // 8, 8, LANES), axis=0)

        def put_first(w, row, v):
            GE1[w, pl.ds(HALO + row, 2 * RB), OWN, :] = v

        def put_seen(w, row, v):
            NAT[w, pl.ds(row, 2 * RB)] = v

        all_wait(XR, 0)
        to_modes(lambda i: XR[i], put_first)
        for w in range(WIDE):
            halo_start(GE1, 0, w)
        send_tile(PS, XS, 1)
        for w in range(WIDE):
            inner(GE1, 0, w)
        for w in range(WIDE):
            outer(GE1, 0, w)
            keep_rows(w, NZ)
            stencil_part(w)
        to_time(lambda w, rows: NZ[w, rows, OWN, :], TZ)
        all_wait(XS, 1)
        to_modes(lambda i: TZ[i] * XS[i], put_seen)

        sums = (zero, zero)
        for w in range(WIDE):
            def first_image(r, acc):
                fit, curve = acc
                zh = NZ[w, r, OWN, :]
                q = NQ[w, r, OWN, :] + NAT[w, r]
                GE2[w, r + HALO, OWN, :] = q
                return fit + fold_cells(GE1[w, r + HALO, OWN, :] * zh), curve + fold_cells(zh * q)

            sums = lax.fori_loop(0, ROWS, first_image, sums)
            halo_start(GE2, 1, w)
        sum_start(0, 0, pack(sums))
        send_days(TZ, FZ, 2)
        to_time(lambda w, rows: GE2[w, pl.ds(rows.start + HALO, rows.size), OWN, :], TQ)
        send_days(TQ, FQ, 3)

        def swap_days(src, dst):
            def one(i, c):
                for r, v in enumerate(swap([src[4 * i + q] for q in range(4)])):
                    dst[i, r] = v
                return c

            lax.fori_loop(0, SLABS, one, 0)

        sum_start(0, 1, sum_end(0, 0))
        for w in range(WIDE):
            inner(GE2, 1, w)
        sum_start(0, 2, sum_end(0, 1))
        for w in range(WIDE):
            outer(GE2, 1, w)
            keep_rows(w, NW)
            if w == 0:
                all_wait(FZ, 2)
                swap_days(FZ, AZ)
            if w + 1 < WIDE:
                stencil_part(w)
        to_time(lambda w, rows: NW[w, rows, OWN, :], TW)
        stencil_part(WIDE - 1)
        fit0, curve0, _ = sum_values(sum_end(0, 2))
        alpha0 = fit0 / curve0

        sums = (zero, zero, zero)
        for w in range(WIDE):
            def second_image(r, acc):
                fit, seen, cross = acc
                wh, g = NW[w, r, OWN, :], GE2[w, r + HALO, OWN, :]
                z1 = NZ[w, r, OWN, :] - alpha0 * wh
                r1 = GE1[w, r + HALO, OWN, :] - alpha0 * g
                return (
                    fit + fold_cells(r1 * z1), seen + fold_cells(z1 * NQ[w, r, OWN, :]),
                    cross + fold_cells(z1 * g),
                )

            sums = lax.fori_loop(0, ROWS, second_image, sums)

        def seen_part(i, acc):
            yt, t = i >> CBITS, pl.multiple_of((i & (NT // COLS - 1)) * COLS, COLS)
            rows = pl.ds(t, COLS)
            tw = TW[yt, rows]
            return acc + fold_cells(XS[yt, rows] * (TZ[yt, rows] - alpha0 * tw) * tw)

        fit, seen, cross = sums
        seen = lax.fori_loop(0, Y * NT // COLS, seen_part, seen)
        sum_start(1, 0, pack((fit, seen, cross)))
        send_days(TW, FW, 4)
        to_time(lambda w, rows: NQ[w, rows, OWN, :], TV, lambda i: XS[i] * TW[i])
        sum_start(1, 1, sum_end(1, 0))
        send_days(TV, FV, 5)
        sum_start(1, 2, sum_end(1, 1))
        all_wait(FQ, 3)
        swap_days(FQ, AQ)
        all_wait(FW, 4)
        swap_days(FW, AW)
        fit1, seen1, cross1 = sum_values(sum_end(1, 2))
        curve1 = cross1 - alpha0 * seen1
        beta = fit1 / fit0
        alpha1 = fit1 / (curve1 + 2.0 * beta * cross1 + beta * beta * curve0)
        c_old = alpha0 + alpha1 + alpha1 * beta
        c_new = alpha0 * alpha1

        def finish_solution(i, c):
            lanes = pl.ds(pl.multiple_of(i * LANES, LANES), LANES)
            for r in range(RB):
                sol_out[r, :, lanes] = c_old * AZ[i, r] - c_new * AW[i, r]
            return c

        def finish_residual(i, c):
            lanes = pl.ds(pl.multiple_of(i * LANES, LANES), LANES)
            for r, v in enumerate(swap([FV[4 * i + q] for q in range(4)])):
                res_out[r, :, lanes] = RL[i, r] - c_old * AQ[i, r] + c_new * v
            return c

        lax.fori_loop(0, SLABS, finish_solution, 0)
        outs = [
            pltpu.make_async_copy(src, dst, out_sem.at[i])
            for i, (src, dst) in enumerate(((sol_out, sol), (res_out, res)))
        ]
        outs[0].start()
        all_wait(FV, 5)
        lax.fori_loop(0, SLABS, finish_residual, 0)
        outs[1].start()

        for at in range(6):
            all_wait_send(at)
        for q in range(4):
            @pl.when(4 * d + q != j)
            def _():
                cell_copy(q).wait_send()
        each_way(3, lambda at: near_copy(at).wait_send())
        for n, ge in enumerate((GE1, GE2)):
            for w in range(WIDE):
                each_way(3, lambda at: halo_copy(ge, n, w, at).wait_send())
        for out in outs:
            out.wait()

    f32 = jnp.float32
    extended = pltpu.VMEM((WIDE, ER, EC, LANES), f32)
    strip = pltpu.VMEM((WIDE, ROWS, EC, LANES), f32)
    flat = pltpu.VMEM((WIDE, ROWS, COLS, LANES), f32)
    fields = pltpu.VMEM((WIDE, ER, K, 8, LANES), f32)
    cell = pltpu.VMEM((ER, K, 8, LANES), f32)
    days = pltpu.VMEM((J, TB, LANES), f32)
    tile = pltpu.VMEM((Y, NT, LANES), f32)
    dma = pltpu.SemaphoreType.DMA
    slab = pltpu.VMEM((SLABS, RB, TB, LANES), f32)
    given = pltpu.VMEM((TB * SLABS * RB, LANES), f32)
    scratch = [
        given, pltpu.VMEM((TB * SLABS * RB, LANES), jnp.int32), pltpu.VMEM((RB, J * COLS), f32),
        pltpu.VMEM((RB, J * COLS), jnp.int32), pltpu.VMEM((NT, NT), f32), pltpu.VMEM((8, NT), f32),
        extended, extended, pltpu.VMEM((2, WIDE, ER, K, 8, LANES), f32),
        fields, fields, cell, fields, pltpu.VMEM((2, ER, EC, LANES), f32),
        pltpu.VMEM((2, K, 8, LANES), f32), flat, strip, strip, strip, days, days, tile, tile,
        tile, tile, tile, tile, days, days, days, days,
        pltpu.VMEM((4, 8, LANES), f32), pltpu.VMEM((Y, 8, LANES), f32),
        pltpu.VMEM((8, LANES), f32), pltpu.VMEM((8, 8, LANES), f32),
        pltpu.VMEM((2, 3, 8, LANES), f32), pltpu.VMEM((2, 3, max(Z, D, Y), 8, LANES), f32),
        pltpu.VMEM((RB, TB, J * COLS), f32), pltpu.VMEM((RB, TB, J * COLS), f32), slab, slab, slab, slab,
        dma((2, WIDE, 8)), dma((2, WIDE, 8)), dma((8,)), dma((8,)), dma((6,)), dma((6,)),
        dma((4,)), dma((Y,)), dma((2, 3)), dma((2, 3)), dma((6,)), dma((2,)),
    ]
    return kernel, scratch


def solution(mesh):
    Z = mesh.shape["rows"] // Y
    D = mesh.shape["days"]
    kernel, scratch = make_kernel(Z, D)
    basis, modal = modal_constants(TB * D)
    slabs = Y * D // 4
    smem = pl.BlockSpec(memory_space=pltpu.SMEM)
    hbm = pl.BlockSpec(memory_space=pl.ANY)

    def by_slab(array):
        array = array.reshape(TB, RB, slabs, LANES)
        return jnp.transpose(array, (0, 2, 1, 3)).reshape(TB * slabs * RB, LANES)

    def body(observations, obs_mask, obs_weight, classes, kappa_table):
        shape = jax.ShapeDtypeStruct((RB, TB, slabs * LANES), jnp.float32)
        sol, res = pl.pallas_call(
            kernel,
            out_shape=(shape, shape),
            in_specs=[hbm] * 4 + [smem] + [hbm] * 2,
            out_specs=(hbm, hbm),
            scratch_shapes=scratch,
            compiler_params=pltpu.CompilerParams(
                collective_id=0, has_side_effects=True, vmem_limit_bytes=56 * 1024 * 1024
            ),
        )(
            by_slab(observations), by_slab(obs_mask), obs_weight, classes, kappa_table,
            jnp.asarray(basis), jnp.asarray(modal),
        )
        return jnp.transpose(sol, (1, 0, 2)), jnp.transpose(res, (1, 0, 2))

    in_specs = (P("days", "rows", None), P("days", "rows", None), P("rows", None), P("rows", None), P())
    out_specs = (P("days", "rows", None), P("days", "rows", None))
    return jax.shard_map(body, mesh=mesh, in_specs=in_specs, out_specs=out_specs, check_vma=False)
```

```python
import math

import jax
import jax.numpy as jnp
import numpy as np
from jax import lax
from jax.experimental import pallas as pl
from jax.experimental.pallas import tpu as pltpu
from jax.sharding import PartitionSpec as P

MESH = pl.DeviceIdType.MESH
DEG = 8
TIME_SHIFT = 0.05
HALF_OBS = 0.5
KAPPA_LOW = 0.02
KAPPA_HIGH = 2.0
WEIGHT_LOW = 0.5
WEIGHT_HIGH = 4.0
STENCIL_SCALE = 6.0
STENCIL_TOP = 16.0 / 3.0

Y = 4
TB = 32
RB = 4
COLS = 32
HALO = 8
K = (COLS + 2 * HALO) // 8
LANES = 128
GROUP = 4


def modal_constants(total):
    order = np.arange(1, total + 1, dtype=np.float64)
    phase = np.outer(order, order) % (2 * (total + 1))
    basis = np.sqrt(2.0 / (total + 1)) * np.sin(np.pi * phase / (total + 1))
    eig = 2.0 + TIME_SHIFT - 2.0 * np.cos(np.pi * order / (total + 1))
    lower = eig * KAPPA_LOW + HALF_OBS * WEIGHT_LOW
    upper = eig * (KAPPA_HIGH + STENCIL_TOP) + HALF_OBS * WEIGHT_HIGH
    centre, spread = 0.5 * (upper + lower), 0.5 * (upper - lower)
    rows = np.zeros((8, total), np.float32)
    for at, row in enumerate(
        (eig / STENCIL_SCALE, 1.0 / centre, centre / spread, 1.0 / spread, STENCIL_SCALE / eig)
    ):
        rows[at] = row
    return basis.astype(np.float32), rows


def make_kernel(Z, D):
    NT = TB * D
    ROWS = RB * Y
    J = Y * D
    WIDE = NT // LANES
    DBITS = D.bit_length() - 1
    CBITS = (NT // COLS).bit_length() - 1
    SLABS = J // 4
    ER, EC = ROWS + 2 * HALO, COLS + 2 * HALO
    OWN = pl.ds(HALO, COLS)

    def kernel(
        obs_in, mask_in, weight_in, classes_in, kappa, basis_in, modal_in, sol, res,
        obs, mask, weight, classes, basis, modal,
        GE1, GE2, U, DX, G, KC, SC, NC, MK, NAT, NQ, NZ, NW, PR, PS, XR, XS,
        TZ, TQ, TW, TV, FZ, FQ, FW, FV, PW, CW, CT, CN, SA, RS, sol_out, res_out, RL, AZ, AQ, AW,
        halo_send, halo_recv, near_send, near_recv, all_send, all_recv, cell_send, cell_recv,
        sum_send, sum_recv, load_sem, out_sem,
    ):
        ri, d = lax.axis_index("rows"), lax.axis_index("days")
        z, y = ri // Y, ri % Y
        j = y * D + (d ^ ((D - 1) * (y & 1)))
        top, bottom, left, right = z == 0, z == Z - 1, j == 0, j == J - 1

        def place(jt):
            yt = jt >> DBITS
            return yt, (jt & (D - 1)) ^ ((D - 1) * (yt & 1))

        def device(zt, jt):
            yt, dt = place(jt)
            return (zt * Y + yt, dt)

        north, south = lax.rem(z + Z - 1, Z), lax.rem(z + 1, Z)
        west, east = lax.rem(j + J - 1, J), lax.rem(j + 1, J)

        CN[...] = jnp.zeros_like(CN)
        loads = [
            pltpu.make_async_copy(src, dst, load_sem.at[i])
            for i, (src, dst) in enumerate((
                (weight_in, weight), (classes_in, classes), (obs_in, obs), (mask_in, mask),
                (basis_in, basis), (modal_in, modal),
            ))
        ]
        for load in loads:
            load.start()

        barrier = pltpu.get_barrier_semaphore()

        def greet(target):
            pl.semaphore_signal(barrier, inc=1, device_id=target, device_id_type=MESH)

        def greet_plane(i, c):
            greet(device(z, ((j + i) & (J - 1))))
            return c

        def greet_column(i, c):
            greet((((z + i) & (Z - 1)) * Y + y, d))
            return c

        lax.fori_loop(1, J, greet_plane, 0)
        lax.fori_loop(1, Z, greet_column, 0)
        for zt in (north, south):
            for jt in (west, east):
                greet(device(zt, jt))

        def full(v):
            return jnp.broadcast_to(v, (8, LANES))

        def swap(parts):
            lane = lax.broadcasted_iota(jnp.int32, parts[0].shape, 1)
            wide, even = lane < 64, (lane // 32) % 2 == 0
            t0 = jnp.where(wide, parts[0], pltpu.roll(parts[2], 64, 1))
            t2 = jnp.where(wide, pltpu.roll(parts[0], 64, 1), parts[2])
            t1 = jnp.where(wide, parts[1], pltpu.roll(parts[3], 64, 1))
            t3 = jnp.where(wide, pltpu.roll(parts[1], 64, 1), parts[3])
            d0 = jnp.where(even, t0, pltpu.roll(t1, 32, 1))
            d1 = jnp.where(even, pltpu.roll(t0, 96, 1), t1)
            d2 = jnp.where(even, t2, pltpu.roll(t3, 32, 1))
            d3 = jnp.where(even, pltpu.roll(t2, 96, 1), t3)
            return d0, d1, d2, d3

        loads[0].wait()
        loads[1].wait()
        slab = pl.ds(pl.multiple_of(d * LANES, LANES), LANES)
        cls = classes[:, slab]
        kap = jnp.zeros((RB, LANES), jnp.float32)
        for level in range(16):
            kap = jnp.where(cls == level, kappa[level], kap)
        own_w = weight[:, slab]
        sub8 = lax.broadcasted_iota(jnp.int32, (8, LANES), 0)
        cells = []
        for r in range(RB):
            w_row = jnp.broadcast_to(own_w[r : r + 1], (8, LANES))
            k_row = jnp.broadcast_to(kap[r : r + 1], (8, LANES))
            cells.append(jnp.where(sub8 == 0, w_row, k_row))
        for q, part in enumerate(swap(cells)):
            PW[q] = part

        def day_rows(i, r, t):
            return pl.ds(t * SLABS * RB + RB * i + r, 8, stride=SLABS * RB)

        def seen_rows(i, r):
            lanes = pl.ds(pl.multiple_of(i * LANES, LANES), LANES)
            seen = [mask[day_rows(i, r, t), :] for t in range(0, TB, 8)]
            return jnp.concatenate(seen, axis=0).astype(jnp.float32) * weight[r : r + 1, lanes]

        for load in loads[2:]:
            load.wait()

        def shuffle_rhs(i, c):
            rhs = []
            for r in range(RB):
                seen = [obs[day_rows(i, r, t), :] for t in range(0, TB, 8)]
                rhs.append(seen_rows(i, r) * jnp.concatenate(seen, axis=0))
                RL[i, r] = rhs[r]
            for q, part in enumerate(swap(rhs)):
                PR[4 * i + q] = part
            return c

        lax.fori_loop(0, SLABS, shuffle_rhs, 0)

        pl.semaphore_wait(barrier, (J - 1) + (Z - 1) + 4)

        def cell_copy(q):
            return pltpu.make_async_remote_copy(
                src_ref=PW.at[q], dst_ref=CW.at[y], send_sem=cell_send.at[q],
                recv_sem=cell_recv.at[y], device_id=device(z, 4 * d + q), device_id_type=MESH,
            )

        def cell_local(q):
            return pltpu.make_async_copy(PW.at[q], CW.at[y], cell_recv.at[y])

        for q in range(4):
            @pl.when(4 * d + q != j)
            def _():
                cell_copy(q).start()

            @pl.when(4 * d + q == j)
            def _():
                cell_local(q).start()

        def to_tile(src, dst, at, i):
            jt = ((j + i) & (J - 1))
            return pltpu.make_async_remote_copy(
                src_ref=src.at[jt], dst_ref=dst.at[y, pl.ds(pl.multiple_of(d * TB, TB), TB)],
                send_sem=all_send.at[at], recv_sem=all_recv.at[at],
                device_id=device(z, jt), device_id_type=MESH,
            )

        def to_days(src, dst, at, i):
            jt = ((j + i) & (J - 1))
            yt, dt = place(jt)
            return pltpu.make_async_remote_copy(
                src_ref=src.at[yt, pl.ds(pl.multiple_of(dt * TB, TB), TB)], dst_ref=dst.at[j],
                send_sem=all_send.at[at], recv_sem=all_recv.at[at],
                device_id=device(z, jt), device_id_type=MESH,
            )

        def send_range(copy, src, dst, at, low, high):
            def one(i, c):
                copy(src, dst, at, i).start()
                return c

            lax.fori_loop(low, high, one, 0)

        def own_tile(src, dst, at):
            pltpu.make_async_copy(
                src.at[j], dst.at[y, pl.ds(pl.multiple_of(d * TB, TB), TB)], all_recv.at[at]
            ).start()

        def own_days(src, dst, at):
            pltpu.make_async_copy(
                src.at[y, pl.ds(pl.multiple_of(d * TB, TB), TB)], dst.at[j], all_recv.at[at]
            ).start()

        def send_tile(src, dst, at):
            send_range(to_tile, src, dst, at, 1, J)
            own_tile(src, dst, at)

        def send_days(src, dst, at):
            send_range(to_days, src, dst, at, 1, J)
            own_days(src, dst, at)

        def all_wait(dst, at):
            pltpu.make_async_copy(dst, dst, all_recv.at[at]).wait()

        def all_wait_send(at):
            pltpu.make_async_copy(
                PR.at[pl.ds(0, J - 1)], PR.at[pl.ds(0, J - 1)], all_send.at[at]
            ).wait()

        SIDES, ENDS = (2, 3), (0, 1, 4, 5, 6, 7)
        ways = []
        for dz, dj in ((-1, 0), (1, 0), (0, -1), (0, 1), (-1, -1), (-1, 1), (1, -1), (1, 1)):
            to_ok, from_ok = True, True
            if dz:
                to_ok, from_ok = (~top, ~bottom) if dz < 0 else (~bottom, ~top)
            if dj:
                a, b = (~left, ~right) if dj < 0 else (~right, ~left)
                to_ok, from_ok = (a, b) if to_ok is True else (to_ok & a, from_ok & b)
            zt = z if dz == 0 else (north if dz < 0 else south)
            jt = j if dj == 0 else (west if dj < 0 else east)
            ways.append((dz, dj, device(zt, jt), to_ok, from_ok))

        def near_copy(at):
            return pltpu.make_async_remote_copy(
                src_ref=CT, dst_ref=CN.at[at], send_sem=near_send.at[at],
                recv_sem=near_recv.at[at], device_id=ways[at][2], device_id_type=MESH,
            )

        def halo_copy(ge, n, w, at):
            dz, dj, target, _, _ = ways[at]
            def span(delta, size):
                if delta == 0:
                    return pl.ds(HALO, size), pl.ds(HALO, size)
                if delta < 0:
                    return pl.ds(HALO, HALO), pl.ds(HALO + size, HALO)
                return pl.ds(size, HALO), pl.ds(0, HALO)

            (rs, rd), (cs, cd) = span(dz, ROWS), span(dj, COLS)
            return pltpu.make_async_remote_copy(
                src_ref=ge.at[w, rs, cs], dst_ref=ge.at[w, rd, cd],
                send_sem=halo_send.at[n, w, at], recv_sem=halo_recv.at[n, w, at],
                device_id=target, device_id_type=MESH,
            )

        def each_way(which, do, among=range(8)):
            for at in among:
                way = ways[at]

                @pl.when(way[which])
                def _():
                    do(at)

        def halo_start(ge, n, w):
            each_way(3, lambda at: halo_copy(ge, n, w, at).start())

        def halo_wait(ge, n, w, among):
            each_way(4, lambda at: halo_copy(ge, n, w, at).wait_recv(), among)

        def send_rhs(i, c):
            to_tile(PR, XR, 0, i).start()
            return c

        lax.fori_loop(1, J, send_rhs, 0)
        own_tile(PR, XR, 0)

        def shuffle_seen(i, c):
            for q, part in enumerate(swap([seen_rows(i, r) for r in range(RB)])):
                PS[4 * i + q] = part
            return c

        lax.fori_loop(0, SLABS, shuffle_seen, 0)

        for cond, rows, cols in (
            (top, pl.ds(0, HALO), pl.ds(0, EC)),
            (bottom, pl.ds(HALO + ROWS, HALO), pl.ds(0, EC)),
            (left, pl.ds(0, ER), pl.ds(0, HALO)),
            (right, pl.ds(0, ER), pl.ds(HALO + COLS, HALO)),
        ):
            @pl.when(cond)
            def _():
                for ge in (GE1, GE2):
                    for w in range(WIDE):
                        ge[w, rows, cols, :] = jnp.zeros((rows.size, cols.size, LANES), jnp.float32)


        for yt in range(Y):
            pltpu.make_async_copy(CW.at[yt], CW.at[yt], cell_recv.at[yt]).wait()
        packed = jnp.zeros((8, LANES), jnp.float32)
        for yt in range(Y):
            for f in range(2):
                packed = jnp.where(sub8 == Y * f + yt, CW[yt][f : f + 1], packed)
        CT[...] = packed
        each_way(3, lambda at: near_copy(at).start())

        column = lax.broadcasted_iota(jnp.int32, (8, LANES), 0) * K
        for k in range(K):
            outside = (left & (column + k < HALO)) | (right & (column + k >= HALO + COLS))
            MK[0, k] = jnp.zeros((8, LANES), jnp.float32)
            MK[1, k] = jnp.where(outside, 0.0, 1.0)

        def spread_tile(source, dz, dj):
            for f, scale, shift in ((0, HALF_OBS, 0.0), (1, STENCIL_SCALE, 36.0)):
                for yt in range(Y):
                    if (dz < 0 and RB * (yt + 1) <= ROWS - HALO) or (dz > 0 and RB * yt >= HALO):
                        continue
                    at = Y * f + yt
                    flat = jnp.broadcast_to(source[at : at + 1], (LANES, LANES)) * scale + shift
                    turned = jnp.transpose(flat).reshape(RB, COLS, LANES)
                    row = HALO + dz * ROWS + RB * yt
                    if dj == 0:
                        NC[f, row : row + RB, OWN, :] = turned
                    elif dj < 0:
                        NC[f, row : row + RB, 0:HALO, :] = turned[:, COLS - HALO :]
                    else:
                        NC[f, row : row + RB, HALO + COLS : EC, :] = turned[:, :HALO]

        spread_tile(packed, 0, 0)
        each_way(4, lambda at: near_copy(at).wait_recv())
        for at, way in enumerate(ways):
            spread_tile(CN[at], -way[0], -way[1])

        inv_eig = [full(modal[4:5, w * LANES : (w + 1) * LANES]) for w in range(WIDE)]

        def interleave_cells(e, c):
            for k in range(K):
                hc = NC[0, e, pl.ds(k, 8, stride=K), :]
                kc = NC[1, e, pl.ds(k, 8, stride=K), :]
                KC[e, k] = kc
                for w in range(WIDE):
                    SC[w, e, k] = hc * inv_eig[w] + kc
            return c

        lax.fori_loop(0, ER, interleave_cells, 0)

        def dot(a, b, dims):
            return lax.dot_general(
                a, b, (dims, ((), ())), precision=lax.Precision.HIGHEST,
                preferred_element_type=jnp.float32,
            )

        def to_modes(tile, put):
            def one(i, c):
                v = jnp.concatenate([tile(2 * i), tile(2 * i + 1)], axis=1)
                h = dot(jnp.transpose(v), basis[...], ((1,), (0,)))
                for w in range(WIDE):
                    put(w, 2 * RB * i, h[:, w * LANES : (w + 1) * LANES].reshape(2 * RB, COLS, LANES))
                return c

            lax.fori_loop(0, Y // 2, one, 0)

        def to_time(get, out, extra=None):
            def one(i, c):
                v = [get(w, pl.ds(2 * RB * i, 2 * RB)).reshape(2 * RB * COLS, LANES) for w in range(WIDE)]
                t = dot(basis[...], jnp.concatenate(v, axis=1), ((1,), (1,)))
                for half in range(2):
                    part = t[:, half * LANES : (half + 1) * LANES]
                    out[2 * i + half] = part if extra is None else part + extra(2 * i + half)
                return c

            lax.fori_loop(0, Y // 2, one, 0)

        def coefficients(w):
            lanes = slice(w * LANES, (w + 1) * LANES)
            return [modal[i : i + 1, lanes] for i in range(4)]

        def rows_of(p, w, first, count):
            above = [U[p, w, first - 1, k] for k in range(K)]
            here = [U[p, w, first, k] for k in range(K)]
            for i in range(count):
                below = [U[p, w, first + 1 + i, k] for k in range(K)]
                b = [4.0 * here[k] + (above[k] + below[k]) for k in range(K)]
                line = [pltpu.roll(b[K - 1], 1, 0)] + b + [pltpu.roll(b[0], 7, 0)]
                yield i, here, [(line[k] + line[k + 2]) + 4.0 * b[k] for k in range(K)]
                above, here = here, below

        def begin(ge, w, low, count):
            ic, ie = full(coefficients(w)[1]), inv_eig[w]

            def one(i, c):
                for e in (low + 2 * i, low + 2 * i + 1):
                    for k in range(K):
                        g = ge[w, e, pl.ds(k, 8, stride=K), :]
                        G[w, e, k] = g * ie
                        u = g * ic
                        U[0, w, e, k] = u
                        DX[w, e, k] = u
                return c

            lax.fori_loop(0, count // 2, one, 0)

        def sweeps(w, rows):
            eig6, _, stretch, inv_spread = coefficients(w)

            def sweep(n, ratio):
                p = n % 2
                ratio_next = 1.0 / (2.0 * stretch - ratio)
                momentum = full(ratio_next * ratio)
                step = full(2.0 * ratio_next * inv_spread * eig6)

                def advance(first, count, edge):
                    for at, v, h in rows_of(p, w, first, count):
                        e = first + at
                        inside = 1
                        if edge:
                            above, below = top & (e < HALO), bottom & (e >= HALO + ROWS)
                            inside = jnp.where(above | below, 0, 1)
                        for k in range(K):
                            dx = step * ((G[w, e, k] - SC[w, e, k] * v[k]) + h[k])
                            dx = (momentum * DX[w, e, k] + dx) * MK[inside, k]
                            DX[w, e, k] = dx
                            U[1 - p, w, e, k] = v[k] + dx

                rows(n, advance)
                return ratio_next

            lax.fori_loop(0, DEG - 1, sweep, 1.0 / stretch)

        def inner(ge, n_halo, w):
            halo_wait(ge, n_halo, w, SIDES)
            begin(ge, w, HALO, ROWS)

            def rows(n, advance):
                def one(i, c):
                    advance(HALO + 1 + n + 2 * i, 2, False)
                    return c

                lax.fori_loop(0, ROWS // 2 - 1 - n, one, 0)

            sweeps(w, rows)

        def outer(ge, n_halo, w):
            halo_wait(ge, n_halo, w, ENDS)
            begin(ge, w, 0, HALO)
            begin(ge, w, HALO + ROWS, HALO)

            def rows(n, advance):
                def one(i, c):
                    upper = n + 1 + GROUP * i
                    lower = ROWS + HALO - 1 - n + GROUP * i - HALO
                    advance(jnp.where(i < HALO // GROUP, upper, lower), GROUP, True)
                    return c

                lax.fori_loop(0, 2 * HALO // GROUP, one, 0)

            sweeps(w, rows)

        def keep_rows(w, keep):
            def one(i, c):
                for r in (2 * i, 2 * i + 1):
                    for k in range(K):
                        keep[w, r, pl.ds(k, 8, stride=K), :] = U[(DEG - 1) % 2, w, r + HALO, k]
                return c

            lax.fori_loop(0, ROWS // 2, one, 0)

        def stencil_part(w):
            eig6 = full(coefficients(w)[0])

            def one(i, c):
                first = GROUP * i
                for at, v, h in rows_of((DEG - 1) % 2, w, first + HALO, GROUP):
                    r = first + at
                    for k in range(K):
                        NQ[w, r, pl.ds(k, 8, stride=K), :] = eig6 * (KC[r + HALO, k] * v[k] - h[k])
                return c

            lax.fori_loop(0, ROWS // GROUP, one, 0)

        def pack(parts):
            out = jnp.zeros((8, LANES), jnp.float32)
            for at, part in enumerate(parts):
                out = jnp.where(sub8 == at, jnp.sum(part, axis=0, keepdims=True), out)
            return out

        stages = (
            (D, d, lambda i: (ri, (d + i) & (D - 1))),
            (Y, y, lambda i: (z * Y + ((y + i) & (Y - 1)), d)),
            (Z, z, lambda i: (((z + i) & (Z - 1)) * Y + y, d)),
        )

        def sum_start(at, stage, value):
            count, me, target = stages[stage]
            SA[at, stage] = value
            RS[at, stage, me] = value

            def one(i, c):
                pltpu.make_async_remote_copy(
                    src_ref=SA.at[at, stage], dst_ref=RS.at[at, stage, me],
                    send_sem=sum_send.at[at, stage], recv_sem=sum_recv.at[at, stage],
                    device_id=target(i), device_id_type=MESH,
                ).start()
                return c

            lax.fori_loop(1, count, one, 0)

        def sum_end(at, stage):
            count = stages[stage][0]
            part = RS.at[at, stage, pl.ds(0, count - 1)]
            for side in (sum_recv, sum_send):
                pltpu.make_async_copy(part, part, side.at[at, stage]).wait()
            total = RS[at, stage, 0]
            for i in range(1, count):
                total = total + RS[at, stage, i]
            return total

        def sum_values(total):
            return [jnp.sum(total[i : i + 1], axis=1, keepdims=True) for i in range(3)]

        zero = jnp.zeros((8, LANES), jnp.float32)

        def fold_cells(v):
            return jnp.sum(v.reshape(COLS // 8, 8, LANES), axis=0)

        def put_first(w, row, v):
            GE1[w, pl.ds(HALO + row, 2 * RB), OWN, :] = v

        def put_seen(w, row, v):
            NAT[w, pl.ds(row, 2 * RB)] = v

        all_wait(XR, 0)
        to_modes(lambda i: XR[i], put_first)
        for w in range(WIDE):
            halo_start(GE1, 0, w)
        send_tile(PS, XS, 1)
        for w in range(WIDE):
            inner(GE1, 0, w)
        for w in range(WIDE):
            outer(GE1, 0, w)
            keep_rows(w, NZ)
            stencil_part(w)
        to_time(lambda w, rows: NZ[w, rows, OWN, :], TZ)
        all_wait(XS, 1)
        to_modes(lambda i: TZ[i] * XS[i], put_seen)

        send_days(TZ, FZ, 2)
        sums = (zero, zero)
        for w in range(WIDE):
            def first_image(r, acc):
                fit, curve = acc
                zh = NZ[w, r, OWN, :]
                q = NQ[w, r, OWN, :] + NAT[w, r]
                GE2[w, r + HALO, OWN, :] = q
                return fit + fold_cells(GE1[w, r + HALO, OWN, :] * zh), curve + fold_cells(zh * q)

            sums = lax.fori_loop(0, ROWS, first_image, sums)
            halo_start(GE2, 1, w)
        sum_start(0, 0, pack(sums))
        to_time(lambda w, rows: GE2[w, pl.ds(rows.start + HALO, rows.size), OWN, :], TQ)
        send_days(TQ, FQ, 3)

        def swap_days(src, dst):
            def one(i, c):
                for r, v in enumerate(swap([src[4 * i + q] for q in range(4)])):
                    dst[i, r] = v
                return c

            lax.fori_loop(0, SLABS, one, 0)

        sum_start(0, 1, sum_end(0, 0))
        for w in range(WIDE):
            inner(GE2, 1, w)
        sum_start(0, 2, sum_end(0, 1))
        for w in range(WIDE):
            outer(GE2, 1, w)
            keep_rows(w, NW)
            if w == 0:
                all_wait(FZ, 2)
                swap_days(FZ, AZ)
            if w + 1 < WIDE:
                stencil_part(w)
        to_time(lambda w, rows: NW[w, rows, OWN, :], TW)
        stencil_part(WIDE - 1)
        fit0, curve0, _ = sum_values(sum_end(0, 2))
        alpha0 = fit0 / curve0

        sums = (zero, zero, zero)
        for w in range(WIDE):
            def second_image(r, acc):
                fit, seen, cross = acc
                wh, g = NW[w, r, OWN, :], GE2[w, r + HALO, OWN, :]
                z1 = NZ[w, r, OWN, :] - alpha0 * wh
                r1 = GE1[w, r + HALO, OWN, :] - alpha0 * g
                return (
                    fit + fold_cells(r1 * z1), seen + fold_cells(z1 * NQ[w, r, OWN, :]),
                    cross + fold_cells(z1 * g),
                )

            sums = lax.fori_loop(0, ROWS, second_image, sums)

        def seen_part(i, acc):
            yt, t = i >> CBITS, pl.multiple_of((i & (NT // COLS - 1)) * COLS, COLS)
            rows = pl.ds(t, COLS)
            tw = TW[yt, rows]
            return acc + fold_cells(XS[yt, rows] * (TZ[yt, rows] - alpha0 * tw) * tw)

        fit, seen, cross = sums
        seen = lax.fori_loop(0, Y * NT // COLS, seen_part, seen)
        sum_start(1, 0, pack((fit, seen, cross)))
        send_days(TW, FW, 4)
        to_time(lambda w, rows: NQ[w, rows, OWN, :], TV, lambda i: XS[i] * TW[i])
        sum_start(1, 1, sum_end(1, 0))
        send_days(TV, FV, 5)
        sum_start(1, 2, sum_end(1, 1))
        all_wait(FQ, 3)
        swap_days(FQ, AQ)
        all_wait(FW, 4)
        swap_days(FW, AW)
        fit1, seen1, cross1 = sum_values(sum_end(1, 2))
        curve1 = cross1 - alpha0 * seen1
        beta = fit1 / fit0
        alpha1 = fit1 / (curve1 + 2.0 * beta * cross1 + beta * beta * curve0)
        c_old = alpha0 + alpha1 + alpha1 * beta
        c_new = alpha0 * alpha1

        def finish_solution(i, c):
            lanes = pl.ds(pl.multiple_of(i * LANES, LANES), LANES)
            for r in range(RB):
                sol_out[r, :, lanes] = c_old * AZ[i, r] - c_new * AW[i, r]
            return c

        def finish_residual(i, c):
            lanes = pl.ds(pl.multiple_of(i * LANES, LANES), LANES)
            for r, v in enumerate(swap([FV[4 * i + q] for q in range(4)])):
                res_out[r, :, lanes] = RL[i, r] - c_old * AQ[i, r] + c_new * v
            return c

        lax.fori_loop(0, SLABS, finish_solution, 0)
        outs = [
            pltpu.make_async_copy(src, dst, out_sem.at[i])
            for i, (src, dst) in enumerate(((sol_out, sol), (res_out, res)))
        ]
        outs[0].start()
        all_wait(FV, 5)
        lax.fori_loop(0, SLABS, finish_residual, 0)
        outs[1].start()

        for at in range(6):
            all_wait_send(at)
        for q in range(4):
            @pl.when(4 * d + q != j)
            def _():
                cell_copy(q).wait_send()
        each_way(3, lambda at: near_copy(at).wait_send())
        for n, ge in enumerate((GE1, GE2)):
            for w in range(WIDE):
                each_way(3, lambda at: halo_copy(ge, n, w, at).wait_send())
        for out in outs:
            out.wait()

    f32 = jnp.float32
    extended = pltpu.VMEM((WIDE, ER, EC, LANES), f32)
    strip = pltpu.VMEM((WIDE, ROWS, EC, LANES), f32)
    flat = pltpu.VMEM((WIDE, ROWS, COLS, LANES), f32)
    fields = pltpu.VMEM((WIDE, ER, K, 8, LANES), f32)
    cell = pltpu.VMEM((ER, K, 8, LANES), f32)
    days = pltpu.VMEM((J, TB, LANES), f32)
    tile = pltpu.VMEM((Y, NT, LANES), f32)
    dma = pltpu.SemaphoreType.DMA
    slab = pltpu.VMEM((SLABS, RB, TB, LANES), f32)
    given = pltpu.VMEM((TB * SLABS * RB, LANES), f32)
    scratch = [
        given, pltpu.VMEM((TB * SLABS * RB, LANES), jnp.int32), pltpu.VMEM((RB, J * COLS), f32),
        pltpu.VMEM((RB, J * COLS), jnp.int32), pltpu.VMEM((NT, NT), f32), pltpu.VMEM((8, NT), f32),
        extended, extended, pltpu.VMEM((2, WIDE, ER, K, 8, LANES), f32),
        fields, fields, cell, fields, pltpu.VMEM((2, ER, EC, LANES), f32),
        pltpu.VMEM((2, K, 8, LANES), f32), flat, strip, strip, strip, days, days, tile, tile,
        tile, tile, tile, tile, days, days, days, days,
        pltpu.VMEM((4, 8, LANES), f32), pltpu.VMEM((Y, 8, LANES), f32),
        pltpu.VMEM((8, LANES), f32), pltpu.VMEM((8, 8, LANES), f32),
        pltpu.VMEM((2, 3, 8, LANES), f32), pltpu.VMEM((2, 3, max(Z, D, Y), 8, LANES), f32),
        pltpu.VMEM((RB, TB, J * COLS), f32), pltpu.VMEM((RB, TB, J * COLS), f32), slab, slab, slab, slab,
        dma((2, WIDE, 8)), dma((2, WIDE, 8)), dma((8,)), dma((8,)), dma((6,)), dma((6,)),
        dma((4,)), dma((Y,)), dma((2, 3)), dma((2, 3)), dma((6,)), dma((2,)),
    ]
    return kernel, scratch


def solution(mesh):
    Z = mesh.shape["rows"] // Y
    D = mesh.shape["days"]
    kernel, scratch = make_kernel(Z, D)
    basis, modal = modal_constants(TB * D)
    slabs = Y * D // 4
    smem = pl.BlockSpec(memory_space=pltpu.SMEM)
    hbm = pl.BlockSpec(memory_space=pl.ANY)

    def by_slab(array):
        array = array.reshape(TB, RB, slabs, LANES)
        return jnp.transpose(array, (0, 2, 1, 3)).reshape(TB * slabs * RB, LANES)

    def body(observations, obs_mask, obs_weight, classes, kappa_table):
        shape = jax.ShapeDtypeStruct((RB, TB, slabs * LANES), jnp.float32)
        sol, res = pl.pallas_call(
            kernel,
            out_shape=(shape, shape),
            in_specs=[hbm] * 4 + [smem] + [hbm] * 2,
            out_specs=(hbm, hbm),
            scratch_shapes=scratch,
            compiler_params=pltpu.CompilerParams(
                collective_id=0, has_side_effects=True, vmem_limit_bytes=56 * 1024 * 1024
            ),
        )(
            by_slab(observations), by_slab(obs_mask), obs_weight, classes, kappa_table,
            jnp.asarray(basis), jnp.asarray(modal),
        )
        return jnp.transpose(sol, (1, 0, 2)), jnp.transpose(res, (1, 0, 2))

    in_specs = (P("days", "rows", None), P("days", "rows", None), P("rows", None), P("rows", None), P())
    out_specs = (P("days", "rows", None), P("days", "rows", None))
    return jax.shard_map(body, mesh=mesh, in_specs=in_specs, out_specs=out_specs, check_vma=False)
```
